32 devices in a mesh: pairs: 8 (over z, y), cols: 4 (over x, core).
Axes of the slice: x: 2, y: 2, z: 4, core: 2. Of those that a mesh axis runs over, the one named last changes fastest.
Arguments:
- state: float32 [2, 64, 64, 16384], P(None, 'pairs', None, 'cols'), may hold values from -6 to 6
- sector_mix: float32 [127, 64, 64], P(None, None, 'cols'), may hold values from -2 to 2
- kerr_rates: float32 [2], replicated, may hold values from 0.002 to 0.02
- column_load: int32 [16384], P('cols'), may hold values from 0 to 255
Outputs:
- evolved: float32 [2, 64, 64, 16384], P(None, 'pairs', None, 'cols')
- moment: float32 [1], replicated
The draws below stay inside these ranges and needn't reach their ends.
All inputs are finite; a program needn't handle non-finite values.
Results may differ from the reference program's by a relative error of at most 0.0003.
Values sent between devices are 32-bit elements; how exact they have to be, the bound alone decides.
A program may use at most 192 MiB of HBM per device.

```python
import math
import jax
import jax.numpy as jnp
import numpy as np
from jax import lax

OPT = 64
THIRD = 64
MEMB = 128
WINDOW = 2
COLS = 16384
SECTORS = 127


def draw_sector_mix(key, part):
    key_off, key_diag = jax.random.split(key, 2)
    shape = (SECTORS, OPT, OPT)
    sector_ids = lax.broadcasted_iota(jnp.int32, shape, 0)
    row_ids = lax.broadcasted_iota(jnp.int32, shape, 1)
    col_ids = lax.broadcasted_iota(jnp.int32, shape, 2)
    sector_size = jnp.minimum(sector_ids, SECTORS - 1 - sector_ids) + 1
    spread = 0.6 / jnp.sqrt(sector_size.astype(jnp.float32))
    off_diagonal = jax.random.normal(key_off, shape, jnp.float32) * spread
    off_diagonal = jnp.clip(off_diagonal, -3.0 * spread, 3.0 * spread)
    diagonal = 1.0 + 0.25 * jax.random.uniform(key_diag, shape, jnp.float32, -1.0, 1.0)
    return jnp.where(row_ids == col_ids, diagonal, off_diagonal)


def plant(entries, rng, least, largest):
    longest = entries.shape.index(max(entries.shape))
    spots = []
    for shift in (0, 1):
        where = [jax.random.randint(jax.random.fold_in(rng, axis), (), 0, length) for axis, length in enumerate(entries.shape)]
        where[longest] = (where[longest] + shift) % entries.shape[longest]
        spots.append(tuple(where))
    return entries.at[spots[0]].set(least).at[spots[1]].set(largest)


def shard_levels(key, extent, shards, smallest, high):
    level = 1.0
    for position, blocks in shards:
        steps = jax.random.uniform(jax.random.fold_in(jax.random.fold_in(key, 6), position), (blocks,), jnp.float32, smallest / len(shards), high / len(shards))
        level = level * jnp.repeat(jnp.exp(steps), extent[position] // blocks).reshape((-1,) + (1,) * (len(extent) - 1 - position))
    return level


def bell_draw(rng, dims, scale, reach, cuts=(), kind=jnp.bfloat16):
    drawn = scale * jax.random.normal(rng, dims, jnp.float32)
    if cuts:
        drawn = drawn * shard_levels(rng, dims, cuts, -0.22, 0.18)
    return jnp.clip(drawn, -reach, reach).astype(kind)


def setup_inputs(seed: int = 0) -> dict:
    seeds = jax.random.split(jax.random.key(seed), 5)
    return {
        "state": bell_draw(seeds[0], (2, OPT, OPT, COLS), 1.0, 6.0, ((1, 8), (3, 4)), jnp.float32),
        "sector_mix": draw_sector_mix(jax.random.fold_in(seeds[4], 71), 0),
        "kerr_rates": jnp.clip(jnp.exp(jax.random.uniform(seeds[2], (2,), jnp.float32, math.log(0.002), math.log(0.02))), 0.002, 0.02),
        "column_load": plant(jax.random.randint(seeds[3], (COLS,), 0, 256), jax.random.fold_in(seeds[3], 1), 0, 255).astype(jnp.int32),
    }


def sector_states(sector):
    low_end = max(0, sector - OPT + 1)
    high_end = min(sector, OPT - 1)
    return np.arange(low_end, high_end + 1)


def reference(state, sector_mix, kerr_rates, column_load):
    flat_state = state.reshape(2, OPT * OPT, COLS)
    pieces = []
    row_lists = []
    for sector in range(SECTORS):
        photon_one = sector_states(sector)
        sector_size = photon_one.shape[0]
        row_ids = (photon_one * OPT + sector - photon_one).astype(np.int32)
        sector_rows = jnp.take(flat_state, jnp.asarray(row_ids), axis=1)
        matrix = sector_mix[sector, :sector_size, :sector_size]
        pieces.append(jnp.einsum("ij,pjc->pic", matrix, sector_rows, precision=lax.Precision.HIGHEST))
        row_lists.append(row_ids)
    stacked = jnp.concatenate(pieces, axis=1)
    inverse = np.argsort(np.concatenate(row_lists)).astype(np.int32)
    mixed = jnp.take(stacked, jnp.asarray(inverse), axis=1).reshape(2, OPT, OPT, COLS)
    real_part = mixed[0]
    imag_part = mixed[1]
    levels = jnp.arange(OPT).astype(jnp.float32)
    loads = column_load.astype(jnp.float32)
    phases = (kerr_rates[0] * levels[:, None] + kerr_rates[1] * levels[None, :])[:, :, None] * loads[None, None, :]
    cosine = jnp.cos(phases)
    sine_part = jnp.sin(phases)
    evolved = jnp.stack([cosine * real_part - sine_part * imag_part, sine_part * real_part + cosine * imag_part])
    third_level = (jnp.arange(COLS) // (MEMB * WINDOW)).astype(jnp.float32)
    weight = (levels + 1.0)[:, None, None] * (third_level + 1.0)[None, None, :]
    summed = jnp.sum(weight * (real_part * real_part + imag_part * imag_part))
    moment = summed / float(OPT * OPT * COLS * OPT * THIRD)
    return evolved, moment.reshape(1)
```

```python
import functools

import jax
import jax.numpy as jnp
from jax import lax
from jax.experimental import pallas as pl
from jax.experimental.pallas import tpu as pltpu
from jax.sharding import PartitionSpec as P

THIRD = 64
MEMB = 128
WINDOW = 2
BAND = 8
LANES = 128
PAD = 8
MESH = pl.DeviceIdType.MESH


def needed(group, p, q, local_one, levels):
    low = p * local_one + q * BAND
    high = low + local_one - 1 + BAND - 1
    return jnp.logical_or(
        jnp.logical_and(group == 0, low <= levels - 1),
        jnp.logical_and(group == 1, high >= levels),
    )


def enter(me, mine, count):
    barrier = pltpu.get_barrier_semaphore()

    def greet(k, carry):
        pl.semaphore_signal(
            barrier, inc=1, device_id=(lax.rem(me + k, count), mine), device_id_type=MESH
        )
        return carry

    lax.fori_loop(1, count, greet, 0)
    pl.semaphore_wait(barrier, count - 1)


def scatter_kernel(count, levels, state_ref, rows_ref, send_sem, recv_sem, own_sem):
    me = lax.axis_index("pairs")
    mine = lax.axis_index("cols")
    local_one = state_ref.shape[1]
    half = count // 2
    width = state_ref.shape[3] // half
    bands = levels // BAND
    enter(me, mine, count)

    def view(dest, q):
        start = pl.multiple_of(lax.rem(dest, half) * width, LANES)
        return state_ref.at[:, :, pl.ds(pl.multiple_of(q * BAND, BAND), BAND), pl.ds(start, width)]

    def place(source, q):
        return rows_ref.at[
            :, pl.ds(source * local_one, local_one), pl.ds(pl.multiple_of(q * BAND, BAND), BAND), :
        ]

    def remote(source, dest, q):
        return pltpu.make_async_remote_copy(
            src_ref=view(dest, q),
            dst_ref=place(source, q),
            send_sem=send_sem.at[dest, q],
            recv_sem=recv_sem.at[source, q],
            device_id=(dest, mine),
            device_id_type=MESH,
        )

    def own(q):
        return pltpu.make_async_copy(view(me, q), place(me, q), own_sem.at[q])

    def each(act):
        def outer(q, carry):
            def inner(k, carry):
                act(q, k)
                return carry

            return lax.fori_loop(1, count, inner, carry)

        lax.fori_loop(0, bands, outer, 0)

    def send(q, k):
        dest = lax.rem(me + k, count)

        @pl.when(needed(dest // half, me, q, local_one, levels))
        def _():
            remote(me, dest, q).start()

    def finish(q, k):
        dest = lax.rem(me + k, count)
        source = lax.rem(me + count - k, count)

        @pl.when(needed(dest // half, me, q, local_one, levels))
        def _():
            remote(me, dest, q).wait_send()

        @pl.when(needed(me // half, source, q, local_one, levels))
        def _():
            remote(source, me, q).wait_recv()

    def own_start(q, carry):
        @pl.when(needed(me // half, me, q, local_one, levels))
        def _():
            own(q).start()

        return carry

    def own_wait(q, carry):
        @pl.when(needed(me // half, me, q, local_one, levels))
        def _():
            own(q).wait()

        return carry

    each(send)
    lax.fori_loop(0, bands, own_start, 0)
    each(finish)
    lax.fori_loop(0, bands, own_wait, 0)


def return_kernel(count, levels, rows_ref, home_ref, send_sem, recv_sem, own_sem):
    me = lax.axis_index("pairs")
    mine = lax.axis_index("cols")
    local_one = home_ref.shape[2]
    half = count // 2
    width = rows_ref.shape[3]
    bands = levels // BAND
    enter(me, mine, count)

    def view(dest, q):
        return rows_ref.at[
            :, pl.ds(dest * local_one, local_one), pl.ds(pl.multiple_of(q * BAND, BAND), BAND), :
        ]

    def place(source, q):
        start = pl.multiple_of(lax.rem(source, half) * width, LANES)
        return home_ref.at[
            source // half, :, :, pl.ds(pl.multiple_of(q * BAND, BAND), BAND), pl.ds(start, width)
        ]

    def remote(source, dest, q):
        return pltpu.make_async_remote_copy(
            src_ref=view(dest, q),
            dst_ref=place(source, q),
            send_sem=send_sem.at[dest, q],
            recv_sem=recv_sem.at[source, q],
            device_id=(dest, mine),
            device_id_type=MESH,
        )

    def own(q):
        return pltpu.make_async_copy(view(me, q), place(me, q), own_sem.at[q])

    def each(act):
        def outer(q, carry):
            def inner(k, carry):
                act(q, k)
                return carry

            return lax.fori_loop(1, count, inner, carry)

        lax.fori_loop(0, bands, outer, 0)

    def send(q, k):
        dest = lax.rem(me + k, count)

        @pl.when(needed(me // half, dest, q, local_one, levels))
        def _():
            remote(me, dest, q).start()

    def finish(q, k):
        dest = lax.rem(me + k, count)
        source = lax.rem(me + count - k, count)

        @pl.when(needed(me // half, dest, q, local_one, levels))
        def _():
            remote(me, dest, q).wait_send()

        @pl.when(needed(source // half, me, q, local_one, levels))
        def _():
            remote(source, me, q).wait_recv()

    def own_start(q, carry):
        @pl.when(needed(me // half, me, q, local_one, levels))
        def _():
            own(q).start()

        return carry

    def own_wait(q, carry):
        @pl.when(needed(me // half, me, q, local_one, levels))
        def _():
            own(q).wait()

        return carry

    each(send)
    lax.fori_loop(0, bands, own_start, 0)
    each(finish)
    lax.fori_loop(0, bands, own_wait, 0)


def mix_kernel(levels, group_ref, mix_ref, rows_ref, mixed_ref, moment_ref, planes, factors):
    group = group_ref[0]
    bands = levels // BAND

    @pl.when(pl.program_id(0) == 0)
    def _():
        planes[...] = jnp.zeros_like(planes)

        def split(t, carry):
            whole = mix_ref[t]
            high = whole.astype(jnp.bfloat16)
            low = (whole - high.astype(jnp.float32)).astype(jnp.bfloat16)
            factors[t] = jnp.concatenate([high, high, low], axis=1)
            return carry

        lax.fori_loop(0, levels, split, 0)

    def move(act, which, stride):
        def level(n1, carry):
            for q in range(bands):
                plane = n1 + q * BAND - which * levels
                position = n1 if which == 0 else levels - 1 - q * BAND

                @pl.when(jnp.logical_and(plane > -BAND, plane < levels))
                def _():
                    start = (plane + PAD) * levels + position
                    for part in range(2):
                        act(part, n1, q, pl.ds(start, BAND, stride=stride))

            return carry

        lax.fori_loop(0, levels, level, 0)

    def put(part, n1, q, where):
        planes[part, where, :] = rows_ref[part, n1, q * BAND : (q + 1) * BAND, :]

    def get(part, n1, q, where):
        mixed_ref[part, n1, q * BAND : (q + 1) * BAND, :] = planes[part, where, :]

    def both(act):
        @pl.when(group == 0)
        def _():
            move(act, 0, levels)

        @pl.when(group == 1)
        def _():
            move(act, 1, levels - 1)

    both(put)
    row_ids = lax.broadcasted_iota(jnp.int32, (levels, 2 * LANES), 0)

    def sector(t, total):
        start = pl.multiple_of((t + PAD) * levels, BAND)
        block = jnp.concatenate(
            [planes[0, pl.ds(start, levels), :], planes[1, pl.ds(start, levels), :]], axis=1
        )
        high = block.astype(jnp.bfloat16)
        low = (block - high.astype(jnp.float32)).astype(jnp.bfloat16)
        found = jnp.dot(
            factors[t],
            jnp.concatenate([high, low, high], axis=0),
            preferred_element_type=jnp.float32,
        )
        size = jnp.where(group == 0, t + 1, levels - 1 - t)
        first = jnp.where(group == 0, 0, t + 1)
        found = jnp.where(row_ids < size, found, 0.0)
        planes[0, pl.ds(start, levels), :] = found[:, :LANES]
        planes[1, pl.ds(start, levels), :] = found[:, LANES:]
        weight = (row_ids + (first + 1)).astype(jnp.float32)
        term = weight * found * found
        for band in range(bands):
            total = total + term[band * BAND : (band + 1) * BAND]
        return total

    total = lax.fori_loop(
        0, levels, sector, jnp.zeros((BAND, 2 * LANES), jnp.float32), unroll=4
    )
    moment_ref[...] = total[:, :LANES] + total[:, LANES:]
    both(get)


def evolve_kernel(levels, offset_ref, one_ref, two_ref, home_ref, evolved_ref):
    offset = offset_ref[0]
    local_one = home_ref.shape[2]
    shape = home_ref.shape[3:]
    n2 = lax.broadcasted_iota(jnp.int32, shape, 0)
    cos_two, sin_two = two_ref[0], two_ref[1]
    for i in range(local_one):
        lower = n2 + (offset + i) < levels
        real = jnp.where(lower, home_ref[0, 0, i], home_ref[1, 0, i])
        imag = jnp.where(lower, home_ref[0, 1, i], home_ref[1, 1, i])
        cos_one, sin_one = one_ref[0, i : i + 1, :], one_ref[1, i : i + 1, :]
        cosine = cos_one * cos_two - sin_one * sin_two
        sine = sin_one * cos_two + cos_one * sin_two
        evolved_ref[0, i] = cosine * real - sine * imag
        evolved_ref[1, i] = sine * real + cosine * imag


def local(state, sector_mix, kerr_rates, column_load):
    full_mix = lax.all_gather(sector_mix, "cols", axis=2, tiled=True)
    count = lax.axis_size("pairs")
    me = lax.axis_index("pairs")
    mine = lax.axis_index("cols")
    _, local_one, levels, columns = state.shape
    half = count // 2
    width = columns // half
    bands = levels // BAND
    group = me // half
    f32 = jnp.float32
    semaphores = [
        pltpu.SemaphoreType.DMA((count, bands)),
        pltpu.SemaphoreType.DMA((count, bands)),
        pltpu.SemaphoreType.DMA((bands,)),
    ]
    anywhere = pl.BlockSpec(memory_space=pl.ANY)

    rows = pl.pallas_call(
        functools.partial(scatter_kernel, count, levels),
        out_shape=jax.ShapeDtypeStruct((2, levels, levels, width), f32),
        in_specs=[anywhere],
        out_specs=anywhere,
        scratch_shapes=semaphores,
        compiler_params=pltpu.CompilerParams(
            collective_id=0, has_side_effects=True, vmem_limit_bytes=56 << 20
        ),
        name="scatter",
    )(state)

    padded = jnp.pad(full_mix, ((0, 2 * levels - full_mix.shape[0]), (0, 0), (0, 0)))
    group_mix = lax.dynamic_slice(padded, (group * levels, 0, 0), (levels, levels, levels))
    mixed, moments = pl.pallas_call(
        functools.partial(mix_kernel, levels),
        grid=(width // LANES,),
        out_shape=(
            jax.ShapeDtypeStruct((2, levels, levels, width), f32),
            jax.ShapeDtypeStruct((BAND, width), f32),
        ),
        in_specs=[
            pl.BlockSpec(memory_space=pltpu.SMEM),
            pl.BlockSpec((levels, levels, levels), lambda c: (0, 0, 0)),
            pl.BlockSpec((2, levels, levels, LANES), lambda c: (0, 0, 0, c)),
        ],
        out_specs=(
            pl.BlockSpec((2, levels, levels, LANES), lambda c: (0, 0, 0, c)),
            pl.BlockSpec((BAND, LANES), lambda c: (0, c)),
        ),
        scratch_shapes=[
            pltpu.VMEM((2, (levels + 2 * PAD) * levels, LANES), f32),
            pltpu.VMEM((levels, levels, 3 * levels), jnp.bfloat16),
        ],
        compiler_params=pltpu.CompilerParams(vmem_limit_bytes=48 << 20),
        name="mix",
    )(group.reshape(1).astype(jnp.int32), group_mix, rows)

    first_column = mine * columns + lax.rem(me, half) * width
    column_ids = first_column + jnp.arange(width, dtype=jnp.int32)
    third_level = (column_ids // (MEMB * WINDOW)).astype(f32)
    partial_term = jnp.sum(moments * (third_level + 1.0)[None, :])
    summed = lax.psum(partial_term, ("pairs", "cols"))
    moment = summed / float(levels * levels * columns * lax.axis_size("cols") * levels * THIRD)

    home = pl.pallas_call(
        functools.partial(return_kernel, count, levels),
        out_shape=jax.ShapeDtypeStruct((2, 2, local_one, levels, columns), f32),
        in_specs=[anywhere],
        out_specs=anywhere,
        scratch_shapes=semaphores,
        compiler_params=pltpu.CompilerParams(
            collective_id=1, has_side_effects=True, vmem_limit_bytes=56 << 20
        ),
        name="give_back",
    )(mixed)

    loads = column_load.astype(f32)
    offset = me * local_one
    levels_one = (offset + jnp.arange(local_one)).astype(f32)
    levels_two = jnp.arange(levels).astype(f32)
    phase_one = (kerr_rates[0] * levels_one)[:, None] * loads[None, :]
    phase_two = (kerr_rates[1] * levels_two)[:, None] * loads[None, :]
    one = jnp.stack([jnp.cos(phase_one), jnp.sin(phase_one)])
    two = jnp.stack([jnp.cos(phase_two), jnp.sin(phase_two)])
    tile = min(columns, 512)
    evolved = pl.pallas_call(
        functools.partial(evolve_kernel, levels),
        grid=(columns // tile,),
        out_shape=jax.ShapeDtypeStruct((2, local_one, levels, columns), f32),
        in_specs=[
            pl.BlockSpec(memory_space=pltpu.SMEM),
            pl.BlockSpec((2, local_one, tile), lambda c: (0, 0, c)),
            pl.BlockSpec((2, levels, tile), lambda c: (0, 0, c)),
            pl.BlockSpec((2, 2, local_one, levels, tile), lambda c: (0, 0, 0, 0, c)),
        ],
        out_specs=pl.BlockSpec((2, local_one, levels, tile), lambda c: (0, 0, 0, c)),
        compiler_params=pltpu.CompilerParams(vmem_limit_bytes=48 << 20),
        name="evolve",
    )(offset.reshape(1).astype(jnp.int32), one, two, home)
    return (evolved, moment.reshape(1))


def solution(mesh):
    placed = (P(None, "pairs", None, "cols"), P(None, None, "cols"), P(), P("cols"))
    return jax.shard_map(
        local,
        mesh=mesh,
        in_specs=placed,
        out_specs=(P(None, "pairs", None, "cols"), P()),
        check_vma=False,
    )
```

```python
import functools

import jax
import jax.numpy as jnp
from jax import lax
from jax.experimental import pallas as pl
from jax.experimental.pallas import tpu as pltpu
from jax.sharding import PartitionSpec as P

THIRD = 64
MEMB = 128
WINDOW = 2
BAND = 8
LANES = 128
CHUNK = 256
MESH = pl.DeviceIdType.MESH


def band_count(group, p, local_one, levels):
    lower = lax.div(levels - 1 - p * local_one, BAND) + 1
    upper = levels // BAND - lax.div(levels + 1 - local_one - p * local_one, BAND)
    return jnp.where(group == 0, lower, upper)


def mix_kernel(
    count, groups, levels,
    state_ref, slab_ref, home_ref, moment_ref,
    rows, slabs, planes, factors, own_moment, pair_moments, col_moments,
    go_sem, come_sem, back_sem, home_sem, own_sem, own_home_sem,
    slab_send, slab_recv, slab_own, mp_send, mp_recv, mc_send, mc_recv,
):
    me = lax.axis_index("pairs")
    mine = lax.axis_index("cols")
    local_one, columns = state_ref.shape[1], state_ref.shape[3]
    half = count // 2
    width = columns // half
    chunk = min(CHUNK, width)
    chunks = width // chunk
    bands = levels // BAND
    depth = slab_ref.shape[1]
    group = lax.div(me, half)

    barrier = pltpu.get_barrier_semaphore()

    def greet_pair(k, carry):
        pl.semaphore_signal(
            barrier, inc=1, device_id=(lax.rem(me + k, count), mine), device_id_type=MESH
        )
        return carry

    def greet_col(k, carry):
        pl.semaphore_signal(
            barrier, inc=1, device_id=(me, lax.rem(mine + k, groups)), device_id_type=MESH
        )
        return carry

    lax.fori_loop(1, count, greet_pair, 0)
    lax.fori_loop(1, groups, greet_col, 0)
    pl.semaphore_wait(barrier, count + groups - 2)

    def at_home(ref, owner, c, n):
        first = lax.div(owner, half) * (levels - n * BAND)
        start = lax.rem(owner, half) * width + c * chunk
        return ref.at[
            :, :, pl.ds(pl.multiple_of(first, BAND), n * BAND),
            pl.ds(pl.multiple_of(start, LANES), chunk),
        ]

    def at_owner(owner, p, c, n):
        first = lax.div(owner, half) * (levels - n * BAND)
        return rows.at[
            :, pl.ds(p * local_one, local_one), pl.ds(pl.multiple_of(first, BAND), n * BAND),
            pl.ds(pl.multiple_of(c * chunk, LANES), chunk),
        ]

    def sized(owner, p, act):
        found = band_count(lax.div(owner, half), p, local_one, levels)
        for n in range(1, bands + 1):
            @pl.when(found == n)
            def _():
                act(n)

    def go(p, owner, c, n):
        return pltpu.make_async_remote_copy(
            src_ref=at_home(state_ref, owner, c, n),
            dst_ref=at_owner(owner, p, c, n),
            send_sem=go_sem.at[owner, c],
            recv_sem=come_sem.at[p, c],
            device_id=(owner, mine),
            device_id_type=MESH,
        )

    def back(owner, p, c, n):
        return pltpu.make_async_remote_copy(
            src_ref=at_owner(owner, p, c, n),
            dst_ref=at_home(home_ref.at[lax.div(owner, half)], owner, c, n),
            send_sem=back_sem.at[p, c],
            recv_sem=home_sem.at[owner, c],
            device_id=(p, mine),
            device_id_type=MESH,
        )

    def own_go(c, n):
        return pltpu.make_async_copy(
            at_home(state_ref, me, c, n), at_owner(me, me, c, n), own_sem.at[c]
        )

    def own_back(c, n):
        return pltpu.make_async_copy(
            at_owner(me, me, c, n), at_home(home_ref.at[group], me, c, n), own_home_sem.at[c]
        )

    def peers(act):
        def body(k, carry):
            act(lax.rem(me + k, count))
            return carry

        lax.fori_loop(1, count, body, 0)

    def col_peers(act):
        def body(k, carry):
            act(lax.rem(mine + k, groups))
            return carry

        lax.fori_loop(1, groups, body, 0)

    def slab_place(col):
        return slabs.at[:, pl.ds(pl.multiple_of(col * depth, BAND), depth), :]

    def slab(source, dest):
        return pltpu.make_async_remote_copy(
            src_ref=slab_ref,
            dst_ref=slab_place(source),
            send_sem=slab_send.at[dest],
            recv_sem=slab_recv.at[source],
            device_id=(me, dest),
            device_id_type=MESH,
        )

    slab_here = pltpu.make_async_copy(slab_ref, slab_place(mine), slab_own)
    col_peers(lambda dest: slab(mine, dest).start())
    slab_here.start()

    def send_chunk(c, carry):
        peers(lambda dest: sized(dest, me, lambda n: go(me, dest, c, n).start()))
        sized(me, me, lambda n: own_go(c, n).start())
        return carry

    lax.fori_loop(0, chunks, send_chunk, 0)

    col_peers(lambda source: slab(source, mine).wait_recv())
    slab_here.wait()

    def turn(i, carry):
        wide = jnp.concatenate(
            [slabs[i], jnp.zeros((LANES - levels, LANES), jnp.float32)], axis=0
        )
        planes[0, pl.ds(i, 2 * levels, stride=levels), :] = wide.T
        return carry

    lax.fori_loop(0, levels, turn, 0)

    def split(t, carry):
        start = pl.multiple_of((group * levels + t) * levels, BAND)
        whole = planes[0, pl.ds(start, levels), :][:, :levels]
        high = whole.astype(jnp.bfloat16)
        low = (whole - high.astype(jnp.float32)).astype(jnp.bfloat16)
        factors[t] = jnp.concatenate([high, high, low], axis=1)
        return carry

    lax.fori_loop(0, levels, split, 0)

    def clear(i, carry):
        start = pl.multiple_of(i * levels, BAND)
        for part in range(2):
            planes[part, pl.ds(start, levels), :] = jnp.zeros((levels, LANES), jnp.float32)
        return carry

    lax.fori_loop(0, 2 * levels, clear, 0)
    own_moment[...] = jnp.zeros_like(own_moment)
    row_ids = lax.broadcasted_iota(jnp.int32, (levels, 2 * LANES), 0)

    def both(act):
        @pl.when(group == 0)
        def _():
            def level(n1, carry):
                act(n1, pl.ds(n1 * (levels + 1), levels, stride=levels))
                return carry

            lax.fori_loop(0, levels, level, 0, unroll=2)

        @pl.when(group == 1)
        def _():
            def level(n1, carry):
                act(n1, pl.ds(n1 * levels + levels - 1, levels, stride=levels - 1))
                return carry

            lax.fori_loop(0, levels, level, 0, unroll=2)

    def mix_tile(start_column):
        lanes = pl.ds(pl.multiple_of(start_column, LANES), LANES)

        def put(n1, where):
            for part in range(2):
                planes[part, where, :] = rows[part, n1, :, lanes]

        def get(n1, where):
            for part in range(2):
                rows[part, n1, :, lanes] = planes[part, where, :]

        both(put)

        def sector(t, total):
            start = pl.multiple_of((group * levels + t) * levels, BAND)
            block = jnp.concatenate(
                [planes[0, pl.ds(start, levels), :], planes[1, pl.ds(start, levels), :]], axis=1
            )
            high = block.astype(jnp.bfloat16)
            low = (block - high.astype(jnp.float32)).astype(jnp.bfloat16)
            found = jnp.dot(
                factors[t],
                jnp.concatenate([high, low, high], axis=0),
                preferred_element_type=jnp.float32,
            )
            size = jnp.where(group == 0, t + 1, levels - 1 - t)
            first = jnp.where(group == 0, 0, t + 1)
            found = jnp.where(row_ids < size, found, 0.0)
            planes[0, pl.ds(start, levels), :] = found[:, :LANES]
            planes[1, pl.ds(start, levels), :] = found[:, LANES:]
            term = (row_ids + (first + 1)).astype(jnp.float32) * found * found
            for band in range(bands):
                total = total + term[band * BAND : (band + 1) * BAND]
            return total

        total = lax.fori_loop(
            0, levels, sector, jnp.zeros((BAND, 2 * LANES), jnp.float32), unroll=4
        )
        column = mine * columns + lax.rem(me, half) * width + start_column
        third = lax.div(column, MEMB * WINDOW).astype(jnp.float32)
        own_moment[...] += (third + 1.0) * (total[:, :LANES] + total[:, LANES:])
        both(get)

    def mix_chunk(c, carry):
        peers(lambda source: sized(me, source, lambda n: go(source, me, c, n).wait_recv()))
        sized(me, me, lambda n: own_go(c, n).wait())

        def tile(i, carry):
            mix_tile(c * chunk + i * LANES)
            return carry

        lax.fori_loop(0, chunk // LANES, tile, 0)
        peers(lambda p: sized(me, p, lambda n: back(me, p, c, n).start()))
        sized(me, me, lambda n: own_back(c, n).start())
        return carry

    lax.fori_loop(0, chunks, mix_chunk, 0)

    def moment_pair(source, dest):
        return pltpu.make_async_remote_copy(
            src_ref=own_moment, dst_ref=pair_moments.at[source],
            send_sem=mp_send.at[dest], recv_sem=mp_recv.at[source],
            device_id=(dest, mine), device_id_type=MESH,
        )

    def moment_col(source, dest):
        return pltpu.make_async_remote_copy(
            src_ref=moment_ref, dst_ref=col_moments.at[source],
            send_sem=mc_send.at[dest], recv_sem=mc_recv.at[source],
            device_id=(me, dest), device_id_type=MESH,
        )

    peers(lambda dest: moment_pair(me, dest).start())
    pair_moments[me] = own_moment[...]
    peers(lambda source: moment_pair(source, me).wait_recv())
    moment_ref[...] = jnp.sum(pair_moments[...], axis=0)
    col_peers(lambda dest: moment_col(mine, dest).start())
    col_moments[mine] = moment_ref[...]
    col_peers(lambda source: moment_col(source, mine).wait_recv())
    col_peers(lambda dest: moment_col(mine, dest).wait_send())
    moment_ref[...] = jnp.sum(col_moments[...], axis=0)

    peers(lambda dest: moment_pair(me, dest).wait_send())
    col_peers(lambda dest: slab(mine, dest).wait_send())

    def finish(c, carry):
        peers(lambda dest: sized(dest, me, lambda n: go(me, dest, c, n).wait_send()))
        peers(lambda p: sized(me, p, lambda n: back(me, p, c, n).wait_send()))
        peers(lambda owner: sized(owner, me, lambda n: back(owner, me, c, n).wait_recv()))
        sized(me, me, lambda n: own_back(c, n).wait())
        return carry

    lax.fori_loop(0, chunks, finish, 0)


def evolve_kernel(levels, offset_ref, one_ref, two_ref, home_ref, evolved_ref):
    offset = offset_ref[0]
    local_one = home_ref.shape[2]
    shape = home_ref.shape[3:]
    n2 = lax.broadcasted_iota(jnp.int32, shape, 0)
    cos_two, sin_two = two_ref[0], two_ref[1]
    for i in range(local_one):
        lower = n2 + (offset + i) < levels
        real = jnp.where(lower, home_ref[0, 0, i], home_ref[1, 0, i])
        imag = jnp.where(lower, home_ref[0, 1, i], home_ref[1, 1, i])
        cos_one, sin_one = one_ref[0, i : i + 1, :], one_ref[1, i : i + 1, :]
        cosine = cos_one * cos_two - sin_one * sin_two
        sine = sin_one * cos_two + cos_one * sin_two
        evolved_ref[0, i] = cosine * real - sine * imag
        evolved_ref[1, i] = sine * real + cosine * imag


def local(state, sector_mix, kerr_rates, column_load):
    count = lax.axis_size("pairs")
    groups = lax.axis_size("cols")
    me = lax.axis_index("pairs")
    _, local_one, levels, columns = state.shape
    half = count // 2
    width = columns // half
    chunks = width // min(CHUNK, width)
    f32 = jnp.float32
    anywhere = pl.BlockSpec(memory_space=pl.ANY)
    tile = (BAND, LANES)
    dma = pltpu.SemaphoreType.DMA

    slab = jnp.pad(
        jnp.transpose(sector_mix, (1, 2, 0)),
        ((0, 0), (0, 0), (0, 2 * levels - sector_mix.shape[0])),
    )
    home, moments = pl.pallas_call(
        functools.partial(mix_kernel, count, groups, levels),
        out_shape=(
            jax.ShapeDtypeStruct((2, 2, local_one, levels, columns), f32),
            jax.ShapeDtypeStruct(tile, f32),
        ),
        in_specs=[anywhere, anywhere],
        out_specs=(anywhere, pl.BlockSpec(memory_space=pltpu.VMEM)),
        scratch_shapes=[
            pltpu.VMEM((2, levels, levels, width), f32),
            pltpu.VMEM((levels, levels, 2 * levels), f32),
            pltpu.VMEM((2, 2 * levels * levels, LANES), f32),
            pltpu.VMEM((levels, levels, 3 * levels), jnp.bfloat16),
            pltpu.VMEM(tile, f32),
            pltpu.VMEM((count,) + tile, f32),
            pltpu.VMEM((groups,) + tile, f32),
            dma((count, chunks)), dma((count, chunks)),
            dma((count, chunks)), dma((count, chunks)),
            dma((chunks,)), dma((chunks,)),
            dma((groups,)), dma((groups,)), dma,
            dma((count,)), dma((count,)), dma((groups,)), dma((groups,)),
        ],
        compiler_params=pltpu.CompilerParams(
            collective_id=0, has_side_effects=True, vmem_limit_bytes=58 << 20
        ),
        name="mix",
    )(state, slab)
    moment = jnp.sum(moments) / float(levels * levels * columns * groups * levels * THIRD)

    loads = column_load.astype(f32)
    offset = me * local_one
    levels_one = (offset + jnp.arange(local_one)).astype(f32)
    levels_two = jnp.arange(levels).astype(f32)
    phase_one = (kerr_rates[0] * levels_one)[:, None] * loads[None, :]
    phase_two = (kerr_rates[1] * levels_two)[:, None] * loads[None, :]
    one = jnp.stack([jnp.cos(phase_one), jnp.sin(phase_one)])
    two = jnp.stack([jnp.cos(phase_two), jnp.sin(phase_two)])
    tile_columns = min(columns, 512)
    evolved = pl.pallas_call(
        functools.partial(evolve_kernel, levels),
        grid=(columns // tile_columns,),
        out_shape=jax.ShapeDtypeStruct((2, local_one, levels, columns), f32),
        in_specs=[
            pl.BlockSpec(memory_space=pltpu.SMEM),
            pl.BlockSpec((2, local_one, tile_columns), lambda c: (0, 0, c)),
            pl.BlockSpec((2, levels, tile_columns), lambda c: (0, 0, c)),
            pl.BlockSpec((2, 2, local_one, levels, tile_columns), lambda c: (0, 0, 0, 0, c)),
        ],
        out_specs=pl.BlockSpec((2, local_one, levels, tile_columns), lambda c: (0, 0, 0, c)),
        compiler_params=pltpu.CompilerParams(vmem_limit_bytes=48 << 20),
        name="evolve",
    )(offset.reshape(1).astype(jnp.int32), one, two, home)
    return (evolved, moment.reshape(1))


def solution(mesh):
    placed = (P(None, "pairs", None, "cols"), P(None, None, "cols"), P(), P("cols"))
    return jax.shard_map(
        local,
        mesh=mesh,
        in_specs=placed,
        out_specs=(P(None, "pairs", None, "cols"), P()),
        check_vma=False,
    )
```

```python
import functools

import jax
import jax.numpy as jnp
from jax import lax
from jax.experimental import pallas as pl
from jax.experimental.pallas import tpu as pltpu
from jax.sharding import PartitionSpec as P

THIRD = 64
MEMB = 128
WINDOW = 2
BAND = 8
LANES = 128
CHUNK = 256
MESH = pl.DeviceIdType.MESH


def band_count(group, p, local_one, levels):
    lower = lax.div(levels - 1 - p * local_one, BAND) + 1
    upper = levels // BAND - lax.div(levels + 1 - local_one - p * local_one, BAND)
    return jnp.where(group == 0, lower, upper)


def turned(tile, by):
    return jnp.concatenate([tile[BAND - by :], tile[: BAND - by]], axis=0)


def joined(take, k, group):
    ids = lax.broadcasted_iota(jnp.int32, take(0).shape, 0)
    kept, moved = take(k), turned(take(BAND - k), BAND - k)
    return jnp.where((ids < BAND - k) == (group == 0), kept, moved)


def mix_kernel(
    count, groups, levels,
    state_ref, slab_ref, home_ref, moment_ref, diag_ref,
    rows, slabs, planes, factors, own_moment, pair_moments, col_moments,
    go_sem, come_sem, back_sem, home_sem, own_sem, own_home_sem,
    slab_send, slab_recv, slab_own, mp_send, mp_recv, mc_send, mc_recv,
    stage=None, tiles=None, packs=None, stage_sem=None, pack_go_sem=None, pack_come_sem=None,
    pack_back_sem=None, pack_home_sem=None, pack_own_sem=None, pack_own_home_sem=None,
):
    packed = stage is not None
    me = lax.axis_index("pairs")
    mine = lax.axis_index("cols")
    local_one, columns = state_ref.shape[1], state_ref.shape[3]
    half = count // 2
    width = columns // half
    chunk = min(CHUNK, width)
    chunks = width // chunk
    bands = levels // BAND
    depth = slab_ref.shape[1]
    group = lax.div(me, half)

    barrier = pltpu.get_barrier_semaphore()

    def greet_pair(k, carry):
        pl.semaphore_signal(
            barrier, inc=1, device_id=(lax.rem(me + k, count), mine), device_id_type=MESH
        )
        return carry

    def greet_col(k, carry):
        pl.semaphore_signal(
            barrier, inc=1, device_id=(me, lax.rem(mine + k, groups)), device_id_type=MESH
        )
        return carry

    lax.fori_loop(1, count, greet_pair, 0)
    lax.fori_loop(1, groups, greet_col, 0)
    pl.semaphore_wait(barrier, count + groups - 2)

    def at_home(ref, owner, c, n):
        first = lax.div(owner, half) * (levels - n * BAND)
        start = lax.rem(owner, half) * width + c * chunk
        return ref.at[
            :, :, pl.ds(pl.multiple_of(first, BAND), n * BAND),
            pl.ds(pl.multiple_of(start, LANES), chunk),
        ]

    def at_owner(owner, p, c, n):
        first = lax.div(owner, half) * (levels - n * BAND)
        return rows.at[
            :, pl.ds(p * local_one, local_one), pl.ds(pl.multiple_of(first, BAND), n * BAND),
            pl.ds(pl.multiple_of(c * chunk, LANES), chunk),
        ]

    def sized(owner, p, act):
        found = band_count(lax.div(owner, half), p, local_one, levels) - int(packed)
        for n in range(1, bands + 1):
            @pl.when(found == n)
            def _():
                act(n)

    def go(p, owner, c, n):
        return pltpu.make_async_remote_copy(
            src_ref=at_home(state_ref, owner, c, n),
            dst_ref=at_owner(owner, p, c, n),
            send_sem=go_sem.at[owner, c],
            recv_sem=come_sem.at[p, c],
            device_id=(owner, mine),
            device_id_type=MESH,
        )

    def back(owner, p, c, n):
        return pltpu.make_async_remote_copy(
            src_ref=at_owner(owner, p, c, n),
            dst_ref=at_home(home_ref.at[lax.div(owner, half)], owner, c, n),
            send_sem=back_sem.at[p, c],
            recv_sem=home_sem.at[owner, c],
            device_id=(p, mine),
            device_id_type=MESH,
        )

    def own_go(c, n):
        return pltpu.make_async_copy(
            at_home(state_ref, me, c, n), at_owner(me, me, c, n), own_sem.at[c]
        )

    def own_back(c, n):
        return pltpu.make_async_copy(
            at_owner(me, me, c, n), at_home(home_ref.at[group], me, c, n), own_home_sem.at[c]
        )

    def columns_of(owner, c):
        start = lax.rem(owner, half) * width + c * chunk
        return pl.ds(pl.multiple_of(start, LANES), chunk)

    def pack_tiles(owner, act):
        if not packed:
            return
        for which in range(2):
            @pl.when(lax.div(owner, half) == which)
            def _():
                act(which)

    def pack_at_owner(p, c, which):
        return packs.at[
            :, p, pl.ds(0, 5 - which), :, pl.ds(pl.multiple_of(c * chunk, LANES), chunk)
        ]

    def pack_at_home(owner, c, which):
        return tiles.at[:, pl.ds(5 * which, 5 - which), :, columns_of(owner, c)]

    def pack_result(owner, c, which):
        return diag_ref.at[which, :, pl.ds(0, 5 - which), :, columns_of(owner, c)]

    def pack_go(p, owner, c, which):
        return pltpu.make_async_remote_copy(
            src_ref=pack_at_home(owner, c, which),
            dst_ref=pack_at_owner(p, c, which),
            send_sem=pack_go_sem.at[owner, c],
            recv_sem=pack_come_sem.at[p, c],
            device_id=(owner, mine),
            device_id_type=MESH,
        )

    def pack_back(owner, p, c, which):
        return pltpu.make_async_remote_copy(
            src_ref=pack_at_owner(p, c, which),
            dst_ref=pack_result(owner, c, which),
            send_sem=pack_back_sem.at[p, c],
            recv_sem=pack_home_sem.at[owner, c],
            device_id=(p, mine),
            device_id_type=MESH,
        )

    def pack_own_go(c, which):
        return pltpu.make_async_copy(
            pack_at_home(me, c, which), pack_at_owner(me, c, which), pack_own_sem.at[c]
        )

    def pack_own_back(c, which):
        return pltpu.make_async_copy(
            pack_at_owner(me, c, which), pack_result(me, c, which), pack_own_home_sem.at[c]
        )

    def peers(act):
        def body(k, carry):
            act(lax.rem(me + k, count))
            return carry

        lax.fori_loop(1, count, body, 0)

    def col_peers(act):
        def body(k, carry):
            act(lax.rem(mine + k, groups))
            return carry

        lax.fori_loop(1, groups, body, 0)

    def slab_place(col):
        return slabs.at[:, pl.ds(pl.multiple_of(col * depth, BAND), depth), :]

    def slab(source, dest):
        return pltpu.make_async_remote_copy(
            src_ref=slab_ref,
            dst_ref=slab_place(source),
            send_sem=slab_send.at[dest],
            recv_sem=slab_recv.at[source],
            device_id=(me, dest),
            device_id_type=MESH,
        )

    slab_here = pltpu.make_async_copy(slab_ref, slab_place(mine), slab_own)
    col_peers(lambda dest: slab(mine, dest).start())
    slab_here.start()

    if packed:
        meet = pl.ds(pl.multiple_of(levels - BAND - me * BAND, BAND), BAND)
        staged = pltpu.make_async_copy(state_ref.at[:, :, meet, :], stage, stage_sem)
        staged.start()
        staged.wait()

        def pack(c, carry):
            lanes = pl.ds(pl.multiple_of(c * chunk, LANES), chunk)
            for part in range(2):
                def take(i):
                    return stage[part, i, :, lanes]

                tiles[part, 0, :, lanes] = take(0)
                for k in range(1, 4):
                    for which in range(2):
                        tiles[part, 4 * which + k, :, lanes] = joined(take, k, which)
                for which in range(2):
                    tiles[part, 4 + 4 * which, :, lanes] = take(4)
            return carry

        lax.fori_loop(0, columns // chunk, pack, 0)

    def send_chunk(c, carry):
        def send(dest):
            sized(dest, me, lambda n: go(me, dest, c, n).start())
            pack_tiles(dest, lambda which: pack_go(me, dest, c, which).start())

        peers(send)
        sized(me, me, lambda n: own_go(c, n).start())
        pack_tiles(me, lambda which: pack_own_go(c, which).start())
        return carry

    lax.fori_loop(0, chunks, send_chunk, 0)

    col_peers(lambda source: slab(source, mine).wait_recv())
    slab_here.wait()

    def turn(i, carry):
        wide = jnp.concatenate(
            [slabs[i], jnp.zeros((LANES - levels, LANES), jnp.float32)], axis=0
        )
        planes[0, pl.ds(i, 2 * levels, stride=levels), :] = wide.T
        return carry

    lax.fori_loop(0, levels, turn, 0)

    def split(t, carry):
        start = pl.multiple_of((group * levels + t) * levels, BAND)
        whole = planes[0, pl.ds(start, levels), :][:, :levels]
        high = whole.astype(jnp.bfloat16)
        low = (whole - high.astype(jnp.float32)).astype(jnp.bfloat16)
        factors[t] = jnp.concatenate([high, high, low], axis=1)
        return carry

    lax.fori_loop(0, levels, split, 0)

    def clear(i, carry):
        start = pl.multiple_of(i * levels, BAND)
        for part in range(2):
            planes[part, pl.ds(start, levels), :] = jnp.zeros((levels, LANES), jnp.float32)
        return carry

    lax.fori_loop(0, 2 * levels, clear, 0)
    own_moment[...] = jnp.zeros_like(own_moment)
    row_ids = lax.broadcasted_iota(jnp.int32, (levels, 2 * LANES), 0)

    def both(act):
        @pl.when(group == 0)
        def _():
            def level(n1, carry):
                act(n1, pl.ds(n1 * (levels + 1), levels, stride=levels))
                return carry

            lax.fori_loop(0, levels, level, 0, unroll=2)

        @pl.when(group == 1)
        def _():
            def level(n1, carry):
                act(n1, pl.ds(n1 * levels + levels - 1, levels, stride=levels - 1))
                return carry

            lax.fori_loop(0, levels, level, 0, unroll=2)

    def mix_tile(start_column):
        lanes = pl.ds(pl.multiple_of(start_column, LANES), LANES)

        def put(n1, where):
            for part in range(2):
                planes[part, where, :] = rows[part, n1, :, lanes]

        def get(n1, where):
            for part in range(2):
                rows[part, n1, :, lanes] = planes[part, where, :]

        both(put)

        def sector(t, total):
            start = pl.multiple_of((group * levels + t) * levels, BAND)
            block = jnp.concatenate(
                [planes[0, pl.ds(start, levels), :], planes[1, pl.ds(start, levels), :]], axis=1
            )
            high = block.astype(jnp.bfloat16)
            low = (block - high.astype(jnp.float32)).astype(jnp.bfloat16)
            found = jnp.dot(
                factors[t],
                jnp.concatenate([high, low, high], axis=0),
                preferred_element_type=jnp.float32,
            )
            size = jnp.where(group == 0, t + 1, levels - 1 - t)
            first = jnp.where(group == 0, 0, t + 1)
            found = jnp.where(row_ids < size, found, 0.0)
            planes[0, pl.ds(start, levels), :] = found[:, :LANES]
            planes[1, pl.ds(start, levels), :] = found[:, LANES:]
            term = (row_ids + (first + 1)).astype(jnp.float32) * found * found
            for band in range(bands):
                total = total + term[band * BAND : (band + 1) * BAND]
            return total

        total = lax.fori_loop(
            0, levels, sector, jnp.zeros((BAND, 2 * LANES), jnp.float32), unroll=4
        )
        column = mine * columns + lax.rem(me, half) * width + start_column
        third = lax.div(column, MEMB * WINDOW).astype(jnp.float32)
        own_moment[...] += (third + 1.0) * (total[:, :LANES] + total[:, LANES:])
        both(get)

    def mix_chunk(c, carry):
        def arrive(source):
            sized(me, source, lambda n: go(source, me, c, n).wait_recv())
            pack_tiles(me, lambda which: pack_go(source, me, c, which).wait_recv())

        peers(arrive)
        sized(me, me, lambda n: own_go(c, n).wait())
        pack_tiles(me, lambda which: pack_own_go(c, which).wait())
        lanes = pl.ds(pl.multiple_of(c * chunk, LANES), chunk)

        def place(p, i, part):
            band = pl.ds(pl.multiple_of(levels - BAND - p * BAND, BAND), BAND)
            return (part, p * BAND + i, band, lanes)

        def unpack(p, carry):
            for part in range(2):
                rows[place(p, 0, part)] = packs[part, p, 0, :, lanes]
                for k in range(1, 4):
                    found = packs[part, p, k - group, :, lanes]
                    rows[place(p, k, part)] = found
                    rows[place(p, BAND - k, part)] = turned(found, k)
                rows[place(p, 4, part)] = packs[part, p, 4 - group, :, lanes]
            return carry

        def repack(p, carry):
            for part in range(2):
                def take(i):
                    return rows[place(p, i, part)]

                packs[part, p, 0, :, lanes] = take(0)
                for k in range(1, 4):
                    packs[part, p, k - group, :, lanes] = joined(take, k, group)
                packs[part, p, 4 - group, :, lanes] = take(4)
            return carry

        if packed:
            lax.fori_loop(0, count, unpack, 0)

        def tile(i, carry):
            mix_tile(c * chunk + i * LANES)
            return carry

        lax.fori_loop(0, chunk // LANES, tile, 0)
        if packed:
            lax.fori_loop(0, count, repack, 0)

        def leave(p):
            sized(me, p, lambda n: back(me, p, c, n).start())
            pack_tiles(me, lambda which: pack_back(me, p, c, which).start())

        peers(leave)
        sized(me, me, lambda n: own_back(c, n).start())
        pack_tiles(me, lambda which: pack_own_back(c, which).start())
        return carry

    lax.fori_loop(0, chunks, mix_chunk, 0)

    def moment_pair(source, dest):
        return pltpu.make_async_remote_copy(
            src_ref=own_moment, dst_ref=pair_moments.at[source],
            send_sem=mp_send.at[dest], recv_sem=mp_recv.at[source],
            device_id=(dest, mine), device_id_type=MESH,
        )

    def moment_col(source, dest):
        return pltpu.make_async_remote_copy(
            src_ref=moment_ref, dst_ref=col_moments.at[source],
            send_sem=mc_send.at[dest], recv_sem=mc_recv.at[source],
            device_id=(me, dest), device_id_type=MESH,
        )

    peers(lambda dest: moment_pair(me, dest).start())
    pair_moments[me] = own_moment[...]
    peers(lambda source: moment_pair(source, me).wait_recv())
    moment_ref[...] = jnp.sum(pair_moments[...], axis=0)
    col_peers(lambda dest: moment_col(mine, dest).start())
    col_moments[mine] = moment_ref[...]
    col_peers(lambda source: moment_col(source, mine).wait_recv())
    col_peers(lambda dest: moment_col(mine, dest).wait_send())
    moment_ref[...] = jnp.sum(col_moments[...], axis=0)

    peers(lambda dest: moment_pair(me, dest).wait_send())
    col_peers(lambda dest: slab(mine, dest).wait_send())

    def finish(c, carry):
        peers(lambda dest: sized(dest, me, lambda n: go(me, dest, c, n).wait_send()))
        peers(lambda p: sized(me, p, lambda n: back(me, p, c, n).wait_send()))
        peers(lambda owner: sized(owner, me, lambda n: back(owner, me, c, n).wait_recv()))
        sized(me, me, lambda n: own_back(c, n).wait())

        def finish_pack(peer):
            pack_tiles(peer, lambda which: pack_go(me, peer, c, which).wait_send())
            pack_tiles(me, lambda which: pack_back(me, peer, c, which).wait_send())
            pack_tiles(peer, lambda which: pack_back(peer, me, c, which).wait_recv())

        if packed:
            peers(finish_pack)
            pack_tiles(me, lambda which: pack_own_back(c, which).wait())
        return carry

    lax.fori_loop(0, chunks, finish, 0)


def evolve_kernel(levels, packed, offset_ref, one_ref, two_ref, home_ref, diag_ref, evolved_ref):
    offset = offset_ref[0]
    local_one = home_ref.shape[2]
    shape = home_ref.shape[3:]
    n2 = lax.broadcasted_iota(jnp.int32, shape, 0)
    cos_two, sin_two = two_ref[0], two_ref[1]
    for i in range(local_one):
        lower = n2 + (offset + i) < levels
        real = jnp.where(lower, home_ref[0, 0, i], home_ref[1, 0, i])
        imag = jnp.where(lower, home_ref[0, 1, i], home_ref[1, 1, i])
        cos_one, sin_one = one_ref[0, i : i + 1, :], one_ref[1, i : i + 1, :]
        cosine = cos_one * cos_two - sin_one * sin_two
        sine = sin_one * cos_two + cos_one * sin_two
        evolved_ref[0, i] = cosine * real - sine * imag
        evolved_ref[1, i] = sine * real + cosine * imag
    if not packed:
        return
    band = pl.ds(pl.multiple_of(levels - BAND - offset, BAND), BAND)
    cos_two, sin_two = two_ref[0, band, :], two_ref[1, band, :]
    ids = lax.broadcasted_iota(jnp.int32, cos_two.shape, 0)
    for i in range(local_one):
        k = min(i, BAND - i)
        found = []
        for part in range(2):
            lower = diag_ref[0, part, k]
            if i == 0:
                found.append(lower)
                continue
            upper = diag_ref[1, part, k - 1]
            if i <= 4:
                found.append(jnp.where(ids < BAND - k, lower, upper))
            else:
                found.append(turned(jnp.where(ids < BAND - k, upper, lower), k))
        real, imag = found
        cos_one, sin_one = one_ref[0, i : i + 1, :], one_ref[1, i : i + 1, :]
        cosine = cos_one * cos_two - sin_one * sin_two
        sine = sin_one * cos_two + cos_one * sin_two
        evolved_ref[0, i, band, :] = cosine * real - sine * imag
        evolved_ref[1, i, band, :] = sine * real + cosine * imag


def local(state, sector_mix, kerr_rates, column_load):
    count = lax.axis_size("pairs")
    groups = lax.axis_size("cols")
    me = lax.axis_index("pairs")
    _, local_one, levels, columns = state.shape
    half = count // 2
    width = columns // half
    chunks = width // min(CHUNK, width)
    f32 = jnp.float32
    anywhere = pl.BlockSpec(memory_space=pl.ANY)
    tile = (BAND, LANES)
    dma = pltpu.SemaphoreType.DMA

    slab = jnp.pad(
        jnp.transpose(sector_mix, (1, 2, 0)),
        ((0, 0), (0, 0), (0, 2 * levels - sector_mix.shape[0])),
    )
    packed = local_one == BAND
    extra = [
        pltpu.VMEM((2, local_one, BAND, columns), f32),
        pltpu.VMEM((2, 9, BAND, columns), f32),
        pltpu.VMEM((2, count, 5, BAND, width), f32),
        dma,
        dma((count, chunks)), dma((count, chunks)),
        dma((count, chunks)), dma((count, chunks)),
        dma((chunks,)), dma((chunks,)),
    ]
    home, moments, diag = pl.pallas_call(
        functools.partial(mix_kernel, count, groups, levels),
        out_shape=(
            jax.ShapeDtypeStruct((2, 2, local_one, levels, columns), f32),
            jax.ShapeDtypeStruct(tile, f32),
            jax.ShapeDtypeStruct((2, 2, 5, BAND, columns), f32),
        ),
        in_specs=[anywhere, anywhere],
        out_specs=(anywhere, pl.BlockSpec(memory_space=pltpu.VMEM), anywhere),
        scratch_shapes=[
            pltpu.VMEM((2, levels, levels, width), f32),
            pltpu.VMEM((levels, levels, 2 * levels), f32),
            pltpu.VMEM((2, 2 * levels * levels, LANES), f32),
            pltpu.VMEM((levels, levels, 3 * levels), jnp.bfloat16),
            pltpu.VMEM(tile, f32),
            pltpu.VMEM((count,) + tile, f32),
            pltpu.VMEM((groups,) + tile, f32),
            dma((count, chunks)), dma((count, chunks)),
            dma((count, chunks)), dma((count, chunks)),
            dma((chunks,)), dma((chunks,)),
            dma((groups,)), dma((groups,)), dma,
            dma((count,)), dma((count,)), dma((groups,)), dma((groups,)),
        ] + (extra if packed else []),
        compiler_params=pltpu.CompilerParams(
            collective_id=0, has_side_effects=True, vmem_limit_bytes=58 << 20
        ),
        name="mix",
    )(state, slab)
    moment = jnp.sum(moments) / float(levels * levels * columns * groups * levels * THIRD)

    loads = column_load.astype(f32)
    offset = me * local_one
    levels_one = (offset + jnp.arange(local_one)).astype(f32)
    levels_two = jnp.arange(levels).astype(f32)
    phase_one = (kerr_rates[0] * levels_one)[:, None] * loads[None, :]
    phase_two = (kerr_rates[1] * levels_two)[:, None] * loads[None, :]
    one = jnp.stack([jnp.cos(phase_one), jnp.sin(phase_one)])
    two = jnp.stack([jnp.cos(phase_two), jnp.sin(phase_two)])
    tile_columns = min(columns, 512)
    evolved = pl.pallas_call(
        functools.partial(evolve_kernel, levels, packed),
        grid=(columns // tile_columns,),
        out_shape=jax.ShapeDtypeStruct((2, local_one, levels, columns), f32),
        in_specs=[
            pl.BlockSpec(memory_space=pltpu.SMEM),
            pl.BlockSpec((2, local_one, tile_columns), lambda c: (0, 0, c)),
            pl.BlockSpec((2, levels, tile_columns), lambda c: (0, 0, c)),
            pl.BlockSpec((2, 2, local_one, levels, tile_columns), lambda c: (0, 0, 0, 0, c)),
            pl.BlockSpec((2, 2, 5, BAND, tile_columns), lambda c: (0, 0, 0, 0, c)),
        ],
        out_specs=pl.BlockSpec((2, local_one, levels, tile_columns), lambda c: (0, 0, 0, c)),
        compiler_params=pltpu.CompilerParams(vmem_limit_bytes=48 << 20),
        name="evolve",
    )(offset.reshape(1).astype(jnp.int32), one, two, home, diag)
    return (evolved, moment.reshape(1))


def solution(mesh):
    placed = (P(None, "pairs", None, "cols"), P(None, None, "cols"), P(), P("cols"))
    return jax.shard_map(
        local,
        mesh=mesh,
        in_specs=placed,
        out_specs=(P(None, "pairs", None, "cols"), P()),
        check_vma=False,
    )
```

```python
import functools

import jax
import jax.numpy as jnp
from jax import lax
from jax.experimental import pallas as pl
from jax.experimental.pallas import tpu as pltpu
from jax.sharding import PartitionSpec as P

THIRD = 64
MEMB = 128
WINDOW = 2
BAND = 8
LANES = 128
CHUNK = 256
MESH = pl.DeviceIdType.MESH


def band_count(group, p, local_one, levels):
    lower = lax.div(levels - 1 - p * local_one, BAND) + 1
    upper = levels // BAND - lax.div(levels + 1 - local_one - p * local_one, BAND)
    return jnp.where(group == 0, lower, upper)


def turned(tile, by):
    return jnp.concatenate([tile[BAND - by :], tile[: BAND - by]], axis=0)


def joined(take, k, group):
    ids = lax.broadcasted_iota(jnp.int32, take(0).shape, 0)
    kept, moved = take(k), turned(take(BAND - k), BAND - k)
    return jnp.where((ids < BAND - k) == (group == 0), kept, moved)


def mix_kernel(
    count, groups, levels,
    state_ref, slab_ref, home_ref, moment_ref, diag_ref,
    rows, slabs, planes, factors, own_moment, pair_moments, col_moments,
    go_sem, come_sem, back_sem, home_sem, own_sem, own_home_sem,
    slab_send, slab_recv, slab_own, mp_send, mp_recv, mc_send, mc_recv,
    stage=None, tiles=None, packs=None, stage_sem=None, pack_go_sem=None, pack_come_sem=None,
    pack_back_sem=None, pack_home_sem=None, pack_own_sem=None, pack_own_home_sem=None,
):
    packed = stage is not None
    me = lax.axis_index("pairs")
    mine = lax.axis_index("cols")
    local_one, columns = state_ref.shape[1], state_ref.shape[3]
    half = count // 2
    width = columns // half
    chunk = min(CHUNK, width)
    chunks = width // chunk
    bands = levels // BAND
    depth = slab_ref.shape[1]
    group = lax.div(me, half)

    if packed:
        meet = pl.ds(pl.multiple_of(levels - BAND - me * BAND, BAND), BAND)
        staged = pltpu.make_async_copy(state_ref.at[:, :, meet, :], stage, stage_sem)
        staged.start()
    barrier = pltpu.get_barrier_semaphore()

    def greet_pair(k, carry):
        pl.semaphore_signal(
            barrier, inc=1, device_id=(lax.rem(me + k, count), mine), device_id_type=MESH
        )
        return carry

    def greet_col(k, carry):
        pl.semaphore_signal(
            barrier, inc=1, device_id=(me, lax.rem(mine + k, groups)), device_id_type=MESH
        )
        return carry

    lax.fori_loop(1, count, greet_pair, 0)
    lax.fori_loop(1, groups, greet_col, 0)
    pl.semaphore_wait(barrier, count + groups - 2)

    def at_home(ref, owner, c, n):
        first = lax.div(owner, half) * (levels - n * BAND)
        start = lax.rem(owner, half) * width + c * chunk
        return ref.at[
            :, :, pl.ds(pl.multiple_of(first, BAND), n * BAND),
            pl.ds(pl.multiple_of(start, LANES), chunk),
        ]

    def at_owner(owner, p, c, n):
        first = lax.div(owner, half) * (levels - n * BAND)
        return rows.at[
            :, pl.ds(p * local_one, local_one), pl.ds(pl.multiple_of(first, BAND), n * BAND),
            pl.ds(pl.multiple_of(c * chunk, LANES), chunk),
        ]

    def sized(owner, p, act):
        found = band_count(lax.div(owner, half), p, local_one, levels) - int(packed)
        for n in range(1, bands + 1):
            @pl.when(found == n)
            def _():
                act(n)

    def result_of(owner):
        return home_ref.at[0 if packed else lax.div(owner, half)]

    def go(p, owner, c, n):
        return pltpu.make_async_remote_copy(
            src_ref=at_home(state_ref, owner, c, n),
            dst_ref=at_owner(owner, p, c, n),
            send_sem=go_sem.at[owner, c],
            recv_sem=come_sem.at[p, c],
            device_id=(owner, mine),
            device_id_type=MESH,
        )

    def back(owner, p, c, n):
        return pltpu.make_async_remote_copy(
            src_ref=at_owner(owner, p, c, n),
            dst_ref=at_home(result_of(owner), owner, c, n),
            send_sem=back_sem.at[p, c],
            recv_sem=home_sem.at[owner, c],
            device_id=(p, mine),
            device_id_type=MESH,
        )

    def own_go(c, n):
        return pltpu.make_async_copy(
            at_home(state_ref, me, c, n), at_owner(me, me, c, n), own_sem.at[c]
        )

    def own_back(c, n):
        return pltpu.make_async_copy(
            at_owner(me, me, c, n), at_home(result_of(me), me, c, n), own_home_sem.at[c]
        )

    def columns_of(owner, c):
        start = lax.rem(owner, half) * width + c * chunk
        return pl.ds(pl.multiple_of(start, LANES), chunk)

    def pack_tiles(owner, act):
        if not packed:
            return
        for which in range(2):
            @pl.when(lax.div(owner, half) == which)
            def _():
                act(which)

    def pack_at_owner(p, c, which):
        return packs.at[
            :, p, pl.ds(0, 5 - which), :, pl.ds(pl.multiple_of(c * chunk, LANES), chunk)
        ]

    def pack_at_home(owner, c, which):
        return tiles.at[:, pl.ds(5 * which, 5 - which), :, columns_of(owner, c)]

    def pack_result(owner, c, which):
        return diag_ref.at[which, :, pl.ds(0, 5 - which), :, columns_of(owner, c)]

    def pack_go(p, owner, c, which):
        return pltpu.make_async_remote_copy(
            src_ref=pack_at_home(owner, c, which),
            dst_ref=pack_at_owner(p, c, which),
            send_sem=pack_go_sem.at[owner, c],
            recv_sem=pack_come_sem.at[p, c],
            device_id=(owner, mine),
            device_id_type=MESH,
        )

    def pack_back(owner, p, c, which):
        return pltpu.make_async_remote_copy(
            src_ref=pack_at_owner(p, c, which),
            dst_ref=pack_result(owner, c, which),
            send_sem=pack_back_sem.at[p, c],
            recv_sem=pack_home_sem.at[owner, c],
            device_id=(p, mine),
            device_id_type=MESH,
        )

    def pack_own_go(c, which):
        return pltpu.make_async_copy(
            pack_at_home(me, c, which), pack_at_owner(me, c, which), pack_own_sem.at[c]
        )

    def pack_own_back(c, which):
        return pltpu.make_async_copy(
            pack_at_owner(me, c, which), pack_result(me, c, which), pack_own_home_sem.at[c]
        )

    def peers(act):
        def body(k, carry):
            act(lax.rem(me + k, count))
            return carry

        lax.fori_loop(1, count, body, 0)

    def col_peers(act):
        def body(k, carry):
            act(lax.rem(mine + k, groups))
            return carry

        lax.fori_loop(1, groups, body, 0)

    def slab_place(col):
        return slabs.at[:, pl.ds(pl.multiple_of(col * depth, BAND), depth), :]

    def slab(source, dest):
        return pltpu.make_async_remote_copy(
            src_ref=slab_ref,
            dst_ref=slab_place(source),
            send_sem=slab_send.at[dest],
            recv_sem=slab_recv.at[source],
            device_id=(me, dest),
            device_id_type=MESH,
        )

    slab_here = pltpu.make_async_copy(slab_ref, slab_place(mine), slab_own)
    col_peers(lambda dest: slab(mine, dest).start())
    slab_here.start()

    def send_bands(c):
        peers(lambda dest: sized(dest, me, lambda n: go(me, dest, c, n).start()))
        sized(me, me, lambda n: own_go(c, n).start())

    def send_packs(c):
        if packed:
            peers(
                lambda dest: pack_tiles(dest, lambda which: pack_go(me, dest, c, which).start())
            )
            pack_tiles(me, lambda which: pack_own_go(c, which).start())

    send_bands(0)
    if packed:
        staged.wait()

        def pack(c, carry):
            lanes = pl.ds(pl.multiple_of(c * chunk, LANES), chunk)
            for part in range(2):
                def take(i):
                    return stage[part, i, :, lanes]

                tiles[part, 0, :, lanes] = take(0)
                for k in range(1, 4):
                    for which in range(2):
                        tiles[part, 4 * which + k, :, lanes] = joined(take, k, which)
                for which in range(2):
                    tiles[part, 4 + 4 * which, :, lanes] = take(4)
            return carry

        lax.fori_loop(0, columns // chunk, pack, 0)

    send_packs(0)

    def send_chunk(c, carry):
        send_bands(c)
        send_packs(c)
        return carry

    lax.fori_loop(1, chunks, send_chunk, 0)

    col_peers(lambda source: slab(source, mine).wait_recv())
    slab_here.wait()

    def turn(i, carry):
        wide = jnp.concatenate(
            [slabs[i], jnp.zeros((LANES - levels, LANES), jnp.float32)], axis=0
        )
        planes[0, pl.ds(i, 2 * levels, stride=levels), :] = wide.T
        return carry

    lax.fori_loop(0, levels, turn, 0)

    def split(t, carry):
        start = pl.multiple_of((group * levels + t) * levels, BAND)
        whole = planes[0, pl.ds(start, levels), :][:, :levels]
        high = whole.astype(jnp.bfloat16)
        low = (whole - high.astype(jnp.float32)).astype(jnp.bfloat16)
        factors[t] = jnp.concatenate([high, high, low], axis=1)
        return carry

    lax.fori_loop(0, levels, split, 0)

    def clear(i, carry):
        start = pl.multiple_of(i * levels, BAND)
        for part in range(2):
            planes[part, pl.ds(start, levels), :] = jnp.zeros((levels, LANES), jnp.float32)
        return carry

    lax.fori_loop(0, 2 * levels, clear, 0)
    own_moment[...] = jnp.zeros_like(own_moment)
    row_ids = lax.broadcasted_iota(jnp.int32, (levels, 2 * LANES), 0)

    def both(act):
        @pl.when(group == 0)
        def _():
            def level(n1, carry):
                act(n1, pl.ds(n1 * (levels + 1), levels, stride=levels))
                return carry

            lax.fori_loop(0, levels, level, 0, unroll=2)

        @pl.when(group == 1)
        def _():
            def level(n1, carry):
                act(n1, pl.ds(n1 * levels + levels - 1, levels, stride=levels - 1))
                return carry

            lax.fori_loop(0, levels, level, 0, unroll=2)

    def mix_tile(start_column):
        lanes = pl.ds(pl.multiple_of(start_column, LANES), LANES)

        def put(n1, where):
            for part in range(2):
                planes[part, where, :] = rows[part, n1, :, lanes]

        def get(n1, where):
            for part in range(2):
                rows[part, n1, :, lanes] = planes[part, where, :]

        both(put)

        def sector(t, total):
            start = pl.multiple_of((group * levels + t) * levels, BAND)
            block = jnp.concatenate(
                [planes[0, pl.ds(start, levels), :], planes[1, pl.ds(start, levels), :]], axis=1
            )
            high = block.astype(jnp.bfloat16)
            low = (block - high.astype(jnp.float32)).astype(jnp.bfloat16)
            found = jnp.dot(
                factors[t],
                jnp.concatenate([high, low, high], axis=0),
                preferred_element_type=jnp.float32,
            )
            size = jnp.where(group == 0, t + 1, levels - 1 - t)
            first = jnp.where(group == 0, 0, t + 1)
            found = jnp.where(row_ids < size, found, 0.0)
            planes[0, pl.ds(start, levels), :] = found[:, :LANES]
            planes[1, pl.ds(start, levels), :] = found[:, LANES:]
            term = (row_ids + (first + 1)).astype(jnp.float32) * found * found
            for band in range(bands):
                total = total + term[band * BAND : (band + 1) * BAND]
            return total

        total = lax.fori_loop(
            0, levels, sector, jnp.zeros((BAND, 2 * LANES), jnp.float32), unroll=4
        )
        column = mine * columns + lax.rem(me, half) * width + start_column
        third = lax.div(column, MEMB * WINDOW).astype(jnp.float32)
        own_moment[...] += (third + 1.0) * (total[:, :LANES] + total[:, LANES:])
        both(get)

    def mix_chunk(c, carry):
        def arrive(source):
            sized(me, source, lambda n: go(source, me, c, n).wait_recv())
            pack_tiles(me, lambda which: pack_go(source, me, c, which).wait_recv())

        peers(arrive)
        sized(me, me, lambda n: own_go(c, n).wait())
        pack_tiles(me, lambda which: pack_own_go(c, which).wait())
        lanes = pl.ds(pl.multiple_of(c * chunk, LANES), chunk)

        def place(p, i, part):
            band = pl.ds(pl.multiple_of(levels - BAND - p * BAND, BAND), BAND)
            return (part, p * BAND + i, band, lanes)

        def unpack(p, carry):
            for part in range(2):
                rows[place(p, 0, part)] = packs[part, p, 0, :, lanes]
                for k in range(1, 4):
                    found = packs[part, p, k - group, :, lanes]
                    rows[place(p, k, part)] = found
                    rows[place(p, BAND - k, part)] = turned(found, k)
                rows[place(p, 4, part)] = packs[part, p, 4 - group, :, lanes]
            return carry

        def repack(p, carry):
            for part in range(2):
                def take(i):
                    return rows[place(p, i, part)]

                packs[part, p, 0, :, lanes] = take(0)
                for k in range(1, 4):
                    packs[part, p, k - group, :, lanes] = joined(take, k, group)
                packs[part, p, 4 - group, :, lanes] = take(4)
            return carry

        if packed:
            lax.fori_loop(0, count, unpack, 0)

        def tile(i, carry):
            mix_tile(c * chunk + i * LANES)
            return carry

        lax.fori_loop(0, chunk // LANES, tile, 0)
        if packed:
            lax.fori_loop(0, count, repack, 0)

        def leave(p):
            sized(me, p, lambda n: back(me, p, c, n).start())
            pack_tiles(me, lambda which: pack_back(me, p, c, which).start())

        peers(leave)
        sized(me, me, lambda n: own_back(c, n).start())
        pack_tiles(me, lambda which: pack_own_back(c, which).start())
        return carry

    lax.fori_loop(0, chunks, mix_chunk, 0)

    def moment_pair(source, dest):
        return pltpu.make_async_remote_copy(
            src_ref=own_moment, dst_ref=pair_moments.at[source],
            send_sem=mp_send.at[dest], recv_sem=mp_recv.at[source],
            device_id=(dest, mine), device_id_type=MESH,
        )

    def moment_col(source, dest):
        return pltpu.make_async_remote_copy(
            src_ref=moment_ref, dst_ref=col_moments.at[source],
            send_sem=mc_send.at[dest], recv_sem=mc_recv.at[source],
            device_id=(me, dest), device_id_type=MESH,
        )

    peers(lambda dest: moment_pair(me, dest).start())
    pair_moments[me] = own_moment[...]
    peers(lambda source: moment_pair(source, me).wait_recv())
    moment_ref[...] = jnp.sum(pair_moments[...], axis=0)
    col_peers(lambda dest: moment_col(mine, dest).start())
    col_moments[mine] = moment_ref[...]
    col_peers(lambda source: moment_col(source, mine).wait_recv())
    col_peers(lambda dest: moment_col(mine, dest).wait_send())
    moment_ref[...] = jnp.sum(col_moments[...], axis=0)

    peers(lambda dest: moment_pair(me, dest).wait_send())
    col_peers(lambda dest: slab(mine, dest).wait_send())

    def finish(c, carry):
        peers(lambda dest: sized(dest, me, lambda n: go(me, dest, c, n).wait_send()))
        peers(lambda p: sized(me, p, lambda n: back(me, p, c, n).wait_send()))
        peers(lambda owner: sized(owner, me, lambda n: back(owner, me, c, n).wait_recv()))
        sized(me, me, lambda n: own_back(c, n).wait())

        def finish_pack(peer):
            pack_tiles(peer, lambda which: pack_go(me, peer, c, which).wait_send())
            pack_tiles(me, lambda which: pack_back(me, peer, c, which).wait_send())
            pack_tiles(peer, lambda which: pack_back(peer, me, c, which).wait_recv())

        if packed:
            peers(finish_pack)
            pack_tiles(me, lambda which: pack_own_back(c, which).wait())
        return carry

    lax.fori_loop(0, chunks, finish, 0)


def evolve_kernel(levels, packed, offset_ref, one_ref, two_ref, home_ref, diag_ref, evolved_ref):
    offset = offset_ref[0]
    local_one = home_ref.shape[2]
    shape = home_ref.shape[3:]
    n2 = lax.broadcasted_iota(jnp.int32, shape, 0)
    cos_two, sin_two = two_ref[0], two_ref[1]
    for i in range(local_one):
        real, imag = home_ref[0, 0, i], home_ref[0, 1, i]
        if not packed:
            lower = n2 + (offset + i) < levels
            real = jnp.where(lower, real, home_ref[1, 0, i])
            imag = jnp.where(lower, imag, home_ref[1, 1, i])
        cos_one, sin_one = one_ref[0, i : i + 1, :], one_ref[1, i : i + 1, :]
        cosine = cos_one * cos_two - sin_one * sin_two
        sine = sin_one * cos_two + cos_one * sin_two
        evolved_ref[0, i] = cosine * real - sine * imag
        evolved_ref[1, i] = sine * real + cosine * imag
    if not packed:
        return
    band = pl.ds(pl.multiple_of(levels - BAND - offset, BAND), BAND)
    cos_two, sin_two = two_ref[0, band, :], two_ref[1, band, :]
    ids = lax.broadcasted_iota(jnp.int32, cos_two.shape, 0)
    for i in range(local_one):
        k = min(i, BAND - i)
        found = []
        for part in range(2):
            lower = diag_ref[0, part, k]
            if i == 0:
                found.append(lower)
                continue
            upper = diag_ref[1, part, k - 1]
            if i <= 4:
                found.append(jnp.where(ids < BAND - k, lower, upper))
            else:
                found.append(turned(jnp.where(ids < BAND - k, upper, lower), k))
        real, imag = found
        cos_one, sin_one = one_ref[0, i : i + 1, :], one_ref[1, i : i + 1, :]
        cosine = cos_one * cos_two - sin_one * sin_two
        sine = sin_one * cos_two + cos_one * sin_two
        evolved_ref[0, i, band, :] = cosine * real - sine * imag
        evolved_ref[1, i, band, :] = sine * real + cosine * imag


def local(state, sector_mix, kerr_rates, column_load):
    count = lax.axis_size("pairs")
    groups = lax.axis_size("cols")
    me = lax.axis_index("pairs")
    _, local_one, levels, columns = state.shape
    half = count // 2
    width = columns // half
    chunks = width // min(CHUNK, width)
    f32 = jnp.float32
    anywhere = pl.BlockSpec(memory_space=pl.ANY)
    tile = (BAND, LANES)
    dma = pltpu.SemaphoreType.DMA

    slab = jnp.pad(
        jnp.transpose(sector_mix, (1, 2, 0)),
        ((0, 0), (0, 0), (0, 2 * levels - sector_mix.shape[0])),
    )
    packed = local_one == BAND
    results = 1 if packed else 2
    extra = [
        pltpu.VMEM((2, local_one, BAND, columns), f32),
        pltpu.VMEM((2, 9, BAND, columns), f32),
        pltpu.VMEM((2, count, 5, BAND, width), f32),
        dma,
        dma((count, chunks)), dma((count, chunks)),
        dma((count, chunks)), dma((count, chunks)),
        dma((chunks,)), dma((chunks,)),
    ]
    home, moments, diag = pl.pallas_call(
        functools.partial(mix_kernel, count, groups, levels),
        out_shape=(
            jax.ShapeDtypeStruct((results, 2, local_one, levels, columns), f32),
            jax.ShapeDtypeStruct(tile, f32),
            jax.ShapeDtypeStruct((2, 2, 5, BAND, columns), f32),
        ),
        in_specs=[anywhere, anywhere],
        out_specs=(anywhere, pl.BlockSpec(memory_space=pltpu.VMEM), anywhere),
        scratch_shapes=[
            pltpu.VMEM((2, levels, levels, width), f32),
            pltpu.VMEM((levels, levels, 2 * levels), f32),
            pltpu.VMEM((2, 2 * levels * levels, LANES), f32),
            pltpu.VMEM((levels, levels, 3 * levels), jnp.bfloat16),
            pltpu.VMEM(tile, f32),
            pltpu.VMEM((count,) + tile, f32),
            pltpu.VMEM((groups,) + tile, f32),
            dma((count, chunks)), dma((count, chunks)),
            dma((count, chunks)), dma((count, chunks)),
            dma((chunks,)), dma((chunks,)),
            dma((groups,)), dma((groups,)), dma,
            dma((count,)), dma((count,)), dma((groups,)), dma((groups,)),
        ] + (extra if packed else []),
        compiler_params=pltpu.CompilerParams(
            collective_id=0, has_side_effects=True, vmem_limit_bytes=58 << 20
        ),
        name="mix",
    )(state, slab)
    moment = jnp.sum(moments) / float(levels * levels * columns * groups * levels * THIRD)

    loads = column_load.astype(f32)
    offset = me * local_one
    levels_one = (offset + jnp.arange(local_one)).astype(f32)
    levels_two = jnp.arange(levels).astype(f32)
    phase_one = (kerr_rates[0] * levels_one)[:, None] * loads[None, :]
    phase_two = (kerr_rates[1] * levels_two)[:, None] * loads[None, :]
    one = jnp.stack([jnp.cos(phase_one), jnp.sin(phase_one)])
    two = jnp.stack([jnp.cos(phase_two), jnp.sin(phase_two)])
    tile_columns = min(columns, 512)
    evolved = pl.pallas_call(
        functools.partial(evolve_kernel, levels, packed),
        grid=(columns // tile_columns,),
        out_shape=jax.ShapeDtypeStruct((2, local_one, levels, columns), f32),
        in_specs=[
            pl.BlockSpec(memory_space=pltpu.SMEM),
            pl.BlockSpec((2, local_one, tile_columns), lambda c: (0, 0, c)),
            pl.BlockSpec((2, levels, tile_columns), lambda c: (0, 0, c)),
            pl.BlockSpec((results, 2, local_one, levels, tile_columns), lambda c: (0, 0, 0, 0, c)),
            pl.BlockSpec((2, 2, 5, BAND, tile_columns), lambda c: (0, 0, 0, 0, c)),
        ],
        out_specs=pl.BlockSpec((2, local_one, levels, tile_columns), lambda c: (0, 0, 0, c)),
        compiler_params=pltpu.CompilerParams(vmem_limit_bytes=48 << 20),
        name="evolve",
    )(offset.reshape(1).astype(jnp.int32), one, two, home, diag)
    return (evolved, moment.reshape(1))


def solution(mesh):
    placed = (P(None, "pairs", None, "cols"), P(None, None, "cols"), P(), P("cols"))
    return jax.shard_map(
        local,
        mesh=mesh,
        in_specs=placed,
        out_specs=(P(None, "pairs", None, "cols"), P()),
        check_vma=False,
    )
```

```python
import functools

import jax
import jax.numpy as jnp
from jax import lax
from jax.experimental import pallas as pl
from jax.experimental.pallas import tpu as pltpu
from jax.sharding import PartitionSpec as P

THIRD = 64
MEMB = 128
WINDOW = 2
BAND = 8
LANES = 128
CHUNK = 128
MESH = pl.DeviceIdType.MESH


def band_count(group, p, local_one, levels):
    lower = lax.div(levels - 1 - p * local_one, BAND) + 1
    upper = levels // BAND - lax.div(levels + 1 - local_one - p * local_one, BAND)
    return jnp.where(group == 0, lower, upper)


def turned(tile, by):
    return jnp.concatenate([tile[BAND - by :], tile[: BAND - by]], axis=0)


def joined(take, k, group):
    ids = lax.broadcasted_iota(jnp.int32, take(0).shape, 0)
    kept, moved = take(k), turned(take(BAND - k), BAND - k)
    return jnp.where((ids < BAND - k) == (group == 0), kept, moved)


def mix_kernel(
    count, groups, levels,
    state_ref, slab_ref, home_ref, moment_ref, diag_ref,
    rows, slabs, planes, factors, own_moment, pair_moments, col_moments,
    go_sem, come_sem, back_sem, home_sem, own_sem, own_home_sem,
    slab_send, slab_recv, slab_own, mp_send, mp_recv, mc_send, mc_recv,
    stage=None, tiles=None, packs=None, stage_sem=None, pack_go_sem=None, pack_come_sem=None,
    pack_back_sem=None, pack_home_sem=None, pack_own_sem=None, pack_own_home_sem=None,
):
    packed = stage is not None
    me = lax.axis_index("pairs")
    mine = lax.axis_index("cols")
    local_one, columns = state_ref.shape[1], state_ref.shape[3]
    half = count // 2
    width = columns // half
    chunk = min(CHUNK, width)
    chunks = width // chunk
    bands = levels // BAND
    depth = slab_ref.shape[1]
    group = lax.div(me, half)

    if packed:
        meet = pl.ds(pl.multiple_of(levels - BAND - me * BAND, BAND), BAND)
        staged = pltpu.make_async_copy(state_ref.at[:, :, meet, :], stage, stage_sem)
        staged.start()
    barrier = pltpu.get_barrier_semaphore()

    def greet_pair(k, carry):
        pl.semaphore_signal(
            barrier, inc=1, device_id=(lax.rem(me + k, count), mine), device_id_type=MESH
        )
        return carry

    def greet_col(k, carry):
        pl.semaphore_signal(
            barrier, inc=1, device_id=(me, lax.rem(mine + k, groups)), device_id_type=MESH
        )
        return carry

    lax.fori_loop(1, count, greet_pair, 0)
    lax.fori_loop(1, groups, greet_col, 0)
    pl.semaphore_wait(barrier, count + groups - 2)

    def at_home(ref, owner, c, n):
        first = lax.div(owner, half) * (levels - n * BAND)
        start = lax.rem(owner, half) * width + c * chunk
        return ref.at[
            :, :, pl.ds(pl.multiple_of(first, BAND), n * BAND),
            pl.ds(pl.multiple_of(start, LANES), chunk),
        ]

    def at_owner(owner, p, c, n):
        first = lax.div(owner, half) * (levels - n * BAND)
        return rows.at[
            :, pl.ds(p * local_one, local_one), pl.ds(pl.multiple_of(first, BAND), n * BAND),
            pl.ds(pl.multiple_of(c * chunk, LANES), chunk),
        ]

    def sized(owner, p, act):
        found = band_count(lax.div(owner, half), p, local_one, levels) - int(packed)
        for n in range(1, bands + 1):
            @pl.when(found == n)
            def _():
                act(n)

    def result_of(owner):
        return home_ref.at[0 if packed else lax.div(owner, half)]

    def go(p, owner, c, n):
        return pltpu.make_async_remote_copy(
            src_ref=at_home(state_ref, owner, c, n),
            dst_ref=at_owner(owner, p, c, n),
            send_sem=go_sem.at[owner, c],
            recv_sem=come_sem.at[p, c],
            device_id=(owner, mine),
            device_id_type=MESH,
        )

    def back(owner, p, c, n):
        return pltpu.make_async_remote_copy(
            src_ref=at_owner(owner, p, c, n),
            dst_ref=at_home(result_of(owner), owner, c, n),
            send_sem=back_sem.at[p, c],
            recv_sem=home_sem.at[owner, c],
            device_id=(p, mine),
            device_id_type=MESH,
        )

    def own_go(c, n):
        return pltpu.make_async_copy(
            at_home(state_ref, me, c, n), at_owner(me, me, c, n), own_sem.at[c]
        )

    def own_back(c, n):
        return pltpu.make_async_copy(
            at_owner(me, me, c, n), at_home(result_of(me), me, c, n), own_home_sem.at[c]
        )

    def columns_of(owner, c):
        start = lax.rem(owner, half) * width + c * chunk
        return pl.ds(pl.multiple_of(start, LANES), chunk)

    def pack_tiles(owner, act):
        if not packed:
            return
        for which in range(2):
            @pl.when(lax.div(owner, half) == which)
            def _():
                act(which)

    def pack_at_owner(p, c, which):
        return packs.at[
            :, p, pl.ds(0, 5 - which), :, pl.ds(pl.multiple_of(c * chunk, LANES), chunk)
        ]

    def pack_at_home(owner, c, which):
        return tiles.at[:, pl.ds(5 * which, 5 - which), :, columns_of(owner, c)]

    def pack_result(owner, c, which):
        return diag_ref.at[which, :, pl.ds(0, 5 - which), :, columns_of(owner, c)]

    def pack_go(p, owner, c, which):
        return pltpu.make_async_remote_copy(
            src_ref=pack_at_home(owner, c, which),
            dst_ref=pack_at_owner(p, c, which),
            send_sem=pack_go_sem.at[owner, c],
            recv_sem=pack_come_sem.at[p, c],
            device_id=(owner, mine),
            device_id_type=MESH,
        )

    def pack_back(owner, p, c, which):
        return pltpu.make_async_remote_copy(
            src_ref=pack_at_owner(p, c, which),
            dst_ref=pack_result(owner, c, which),
            send_sem=pack_back_sem.at[p, c],
            recv_sem=pack_home_sem.at[owner, c],
            device_id=(p, mine),
            device_id_type=MESH,
        )

    def pack_own_go(c, which):
        return pltpu.make_async_copy(
            pack_at_home(me, c, which), pack_at_owner(me, c, which), pack_own_sem.at[c]
        )

    def pack_own_back(c, which):
        return pltpu.make_async_copy(
            pack_at_owner(me, c, which), pack_result(me, c, which), pack_own_home_sem.at[c]
        )

    def peers(act):
        def body(k, carry):
            act(lax.rem(me + k, count))
            return carry

        lax.fori_loop(1, count, body, 0)

    def col_peers(act):
        def body(k, carry):
            act(lax.rem(mine + k, groups))
            return carry

        lax.fori_loop(1, groups, body, 0)

    def slab_place(col):
        return slabs.at[:, pl.ds(pl.multiple_of(col * depth, BAND), depth), :]

    def slab(source, dest):
        return pltpu.make_async_remote_copy(
            src_ref=slab_ref,
            dst_ref=slab_place(source),
            send_sem=slab_send.at[dest],
            recv_sem=slab_recv.at[source],
            device_id=(me, dest),
            device_id_type=MESH,
        )

    slab_here = pltpu.make_async_copy(slab_ref, slab_place(mine), slab_own)
    col_peers(lambda dest: slab(mine, dest).start())
    slab_here.start()

    if packed:
        staged.wait()

        def pack(c, carry):
            lanes = pl.ds(pl.multiple_of(c * chunk, LANES), chunk)
            for part in range(2):
                def take(i):
                    return stage[part, i, :, lanes]

                tiles[part, 0, :, lanes] = take(0)
                for k in range(1, 4):
                    for which in range(2):
                        tiles[part, 4 * which + k, :, lanes] = joined(take, k, which)
                for which in range(2):
                    tiles[part, 4 + 4 * which, :, lanes] = take(4)
            return carry

        lax.fori_loop(0, columns // chunk, pack, 0)

    def send_chunk(c, carry):
        def send(dest):
            sized(dest, me, lambda n: go(me, dest, c, n).start())
            pack_tiles(dest, lambda which: pack_go(me, dest, c, which).start())

        peers(send)
        sized(me, me, lambda n: own_go(c, n).start())
        pack_tiles(me, lambda which: pack_own_go(c, which).start())
        return carry

    lax.fori_loop(0, chunks, send_chunk, 0)

    col_peers(lambda source: slab(source, mine).wait_recv())
    slab_here.wait()

    def turn(i, carry):
        wide = jnp.concatenate(
            [slabs[i], jnp.zeros((LANES - levels, LANES), jnp.float32)], axis=0
        )
        planes[0, pl.ds(i, 2 * levels, stride=levels), :] = wide.T
        return carry

    lax.fori_loop(0, levels, turn, 0)

    def split(t, carry):
        start = pl.multiple_of((group * levels + t) * levels, BAND)
        whole = planes[0, pl.ds(start, levels), :][:, :levels]
        high = whole.astype(jnp.bfloat16)
        low = (whole - high.astype(jnp.float32)).astype(jnp.bfloat16)
        factors[t] = jnp.concatenate([high, high, low], axis=1)
        return carry

    lax.fori_loop(0, levels, split, 0)

    def clear(i, carry):
        start = pl.multiple_of(i * levels, BAND)
        for part in range(2):
            planes[part, pl.ds(start, levels), :] = jnp.zeros((levels, LANES), jnp.float32)
        return carry

    lax.fori_loop(0, 2 * levels, clear, 0)
    own_moment[...] = jnp.zeros_like(own_moment)
    row_ids = lax.broadcasted_iota(jnp.int32, (levels, 2 * LANES), 0)

    def both(act):
        @pl.when(group == 0)
        def _():
            def level(n1, carry):
                act(n1, pl.ds(n1 * (levels + 1), levels, stride=levels))
                return carry

            lax.fori_loop(0, levels, level, 0, unroll=2)

        @pl.when(group == 1)
        def _():
            def level(n1, carry):
                act(n1, pl.ds(n1 * levels + levels - 1, levels, stride=levels - 1))
                return carry

            lax.fori_loop(0, levels, level, 0, unroll=2)

    def mix_tile(start_column):
        lanes = pl.ds(pl.multiple_of(start_column, LANES), LANES)

        def put(n1, where):
            for part in range(2):
                planes[part, where, :] = rows[part, n1, :, lanes]

        def get(n1, where):
            for part in range(2):
                rows[part, n1, :, lanes] = planes[part, where, :]

        both(put)

        def sector(t, total):
            start = pl.multiple_of((group * levels + t) * levels, BAND)
            block = jnp.concatenate(
                [planes[0, pl.ds(start, levels), :], planes[1, pl.ds(start, levels), :]], axis=1
            )
            high = block.astype(jnp.bfloat16)
            low = (block - high.astype(jnp.float32)).astype(jnp.bfloat16)
            found = jnp.dot(
                factors[t],
                jnp.concatenate([high, low, high], axis=0),
                preferred_element_type=jnp.float32,
            )
            size = jnp.where(group == 0, t + 1, levels - 1 - t)
            first = jnp.where(group == 0, 0, t + 1)
            found = jnp.where(row_ids < size, found, 0.0)
            planes[0, pl.ds(start, levels), :] = found[:, :LANES]
            planes[1, pl.ds(start, levels), :] = found[:, LANES:]
            term = (row_ids + (first + 1)).astype(jnp.float32) * found * found
            for band in range(bands):
                total = total + term[band * BAND : (band + 1) * BAND]
            return total

        total = lax.fori_loop(
            0, levels, sector, jnp.zeros((BAND, 2 * LANES), jnp.float32), unroll=4
        )
        column = mine * columns + lax.rem(me, half) * width + start_column
        third = lax.div(column, MEMB * WINDOW).astype(jnp.float32)
        own_moment[...] += (third + 1.0) * (total[:, :LANES] + total[:, LANES:])
        both(get)

    def mix_chunk(c, carry):
        def arrive(source):
            sized(me, source, lambda n: go(source, me, c, n).wait_recv())
            pack_tiles(me, lambda which: pack_go(source, me, c, which).wait_recv())

        peers(arrive)
        sized(me, me, lambda n: own_go(c, n).wait())
        pack_tiles(me, lambda which: pack_own_go(c, which).wait())
        lanes = pl.ds(pl.multiple_of(c * chunk, LANES), chunk)

        def place(p, i, part):
            band = pl.ds(pl.multiple_of(levels - BAND - p * BAND, BAND), BAND)
            return (part, p * BAND + i, band, lanes)

        def unpack(p, carry):
            for part in range(2):
                rows[place(p, 0, part)] = packs[part, p, 0, :, lanes]
                for k in range(1, 4):
                    found = packs[part, p, k - group, :, lanes]
                    rows[place(p, k, part)] = found
                    rows[place(p, BAND - k, part)] = turned(found, k)
                rows[place(p, 4, part)] = packs[part, p, 4 - group, :, lanes]
            return carry

        def repack(p, carry):
            for part in range(2):
                def take(i):
                    return rows[place(p, i, part)]

                packs[part, p, 0, :, lanes] = take(0)
                for k in range(1, 4):
                    packs[part, p, k - group, :, lanes] = joined(take, k, group)
                packs[part, p, 4 - group, :, lanes] = take(4)
            return carry

        if packed:
            lax.fori_loop(0, count, unpack, 0)

        def tile(i, carry):
            mix_tile(c * chunk + i * LANES)
            return carry

        lax.fori_loop(0, chunk // LANES, tile, 0)
        if packed:
            lax.fori_loop(0, count, repack, 0)

        def leave(p):
            sized(me, p, lambda n: back(me, p, c, n).start())
            pack_tiles(me, lambda which: pack_back(me, p, c, which).start())

        peers(leave)
        sized(me, me, lambda n: own_back(c, n).start())
        pack_tiles(me, lambda which: pack_own_back(c, which).start())
        return carry

    lax.fori_loop(0, chunks, mix_chunk, 0)

    def moment_pair(source, dest):
        return pltpu.make_async_remote_copy(
            src_ref=own_moment, dst_ref=pair_moments.at[source],
            send_sem=mp_send.at[dest], recv_sem=mp_recv.at[source],
            device_id=(dest, mine), device_id_type=MESH,
        )

    def moment_col(source, dest):
        return pltpu.make_async_remote_copy(
            src_ref=moment_ref, dst_ref=col_moments.at[source],
            send_sem=mc_send.at[dest], recv_sem=mc_recv.at[source],
            device_id=(me, dest), device_id_type=MESH,
        )

    peers(lambda dest: moment_pair(me, dest).start())
    pair_moments[me] = own_moment[...]
    peers(lambda source: moment_pair(source, me).wait_recv())
    moment_ref[...] = jnp.sum(pair_moments[...], axis=0)
    col_peers(lambda dest: moment_col(mine, dest).start())
    col_moments[mine] = moment_ref[...]
    col_peers(lambda source: moment_col(source, mine).wait_recv())
    col_peers(lambda dest: moment_col(mine, dest).wait_send())
    moment_ref[...] = jnp.sum(col_moments[...], axis=0)

    peers(lambda dest: moment_pair(me, dest).wait_send())
    col_peers(lambda dest: slab(mine, dest).wait_send())

    def finish(c, carry):
        peers(lambda dest: sized(dest, me, lambda n: go(me, dest, c, n).wait_send()))
        peers(lambda p: sized(me, p, lambda n: back(me, p, c, n).wait_send()))
        peers(lambda owner: sized(owner, me, lambda n: back(owner, me, c, n).wait_recv()))
        sized(me, me, lambda n: own_back(c, n).wait())

        def finish_pack(peer):
            pack_tiles(peer, lambda which: pack_go(me, peer, c, which).wait_send())
            pack_tiles(me, lambda which: pack_back(me, peer, c, which).wait_send())
            pack_tiles(peer, lambda which: pack_back(peer, me, c, which).wait_recv())

        if packed:
            peers(finish_pack)
            pack_tiles(me, lambda which: pack_own_back(c, which).wait())
        return carry

    lax.fori_loop(0, chunks, finish, 0)


def evolve_kernel(levels, packed, offset_ref, one_ref, two_ref, home_ref, diag_ref, evolved_ref):
    offset = offset_ref[0]
    local_one = home_ref.shape[2]
    shape = home_ref.shape[3:]
    n2 = lax.broadcasted_iota(jnp.int32, shape, 0)
    cos_two, sin_two = two_ref[0], two_ref[1]
    for i in range(local_one):
        real, imag = home_ref[0, 0, i], home_ref[0, 1, i]
        if not packed:
            lower = n2 + (offset + i) < levels
            real = jnp.where(lower, real, home_ref[1, 0, i])
            imag = jnp.where(lower, imag, home_ref[1, 1, i])
        cos_one, sin_one = one_ref[0, i : i + 1, :], one_ref[1, i : i + 1, :]
        cosine = cos_one * cos_two - sin_one * sin_two
        sine = sin_one * cos_two + cos_one * sin_two
        evolved_ref[0, i] = cosine * real - sine * imag
        evolved_ref[1, i] = sine * real + cosine * imag
    if not packed:
        return
    band = pl.ds(pl.multiple_of(levels - BAND - offset, BAND), BAND)
    cos_two, sin_two = two_ref[0, band, :], two_ref[1, band, :]
    ids = lax.broadcasted_iota(jnp.int32, cos_two.shape, 0)
    for i in range(local_one):
        k = min(i, BAND - i)
        found = []
        for part in range(2):
            lower = diag_ref[0, part, k]
            if i == 0:
                found.append(lower)
                continue
            upper = diag_ref[1, part, k - 1]
            if i <= 4:
                found.append(jnp.where(ids < BAND - k, lower, upper))
            else:
                found.append(turned(jnp.where(ids < BAND - k, upper, lower), k))
        real, imag = found
        cos_one, sin_one = one_ref[0, i : i + 1, :], one_ref[1, i : i + 1, :]
        cosine = cos_one * cos_two - sin_one * sin_two
        sine = sin_one * cos_two + cos_one * sin_two
        evolved_ref[0, i, band, :] = cosine * real - sine * imag
        evolved_ref[1, i, band, :] = sine * real + cosine * imag


def local(state, sector_mix, kerr_rates, column_load):
    count = lax.axis_size("pairs")
    groups = lax.axis_size("cols")
    me = lax.axis_index("pairs")
    _, local_one, levels, columns = state.shape
    half = count // 2
    width = columns // half
    chunks = width // min(CHUNK, width)
    f32 = jnp.float32
    anywhere = pl.BlockSpec(memory_space=pl.ANY)
    tile = (BAND, LANES)
    dma = pltpu.SemaphoreType.DMA

    slab = jnp.pad(
        jnp.transpose(sector_mix, (1, 2, 0)),
        ((0, 0), (0, 0), (0, 2 * levels - sector_mix.shape[0])),
    )
    packed = local_one == BAND
    results = 1 if packed else 2
    extra = [
        pltpu.VMEM((2, local_one, BAND, columns), f32),
        pltpu.VMEM((2, 9, BAND, columns), f32),
        pltpu.VMEM((2, count, 5, BAND, width), f32),
        dma,
        dma((count, chunks)), dma((count, chunks)),
        dma((count, chunks)), dma((count, chunks)),
        dma((chunks,)), dma((chunks,)),
    ]
    home, moments, diag = pl.pallas_call(
        functools.partial(mix_kernel, count, groups, levels),
        out_shape=(
            jax.ShapeDtypeStruct((results, 2, local_one, levels, columns), f32),
            jax.ShapeDtypeStruct(tile, f32),
            jax.ShapeDtypeStruct((2, 2, 5, BAND, columns), f32),
        ),
        in_specs=[anywhere, anywhere],
        out_specs=(anywhere, pl.BlockSpec(memory_space=pltpu.VMEM), anywhere),
        scratch_shapes=[
            pltpu.VMEM((2, levels, levels, width), f32),
            pltpu.VMEM((levels, levels, 2 * levels), f32),
            pltpu.VMEM((2, 2 * levels * levels, LANES), f32),
            pltpu.VMEM((levels, levels, 3 * levels), jnp.bfloat16),
            pltpu.VMEM(tile, f32),
            pltpu.VMEM((count,) + tile, f32),
            pltpu.VMEM((groups,) + tile, f32),
            dma((count, chunks)), dma((count, chunks)),
            dma((count, chunks)), dma((count, chunks)),
            dma((chunks,)), dma((chunks,)),
            dma((groups,)), dma((groups,)), dma,
            dma((count,)), dma((count,)), dma((groups,)), dma((groups,)),
        ] + (extra if packed else []),
        compiler_params=pltpu.CompilerParams(
            collective_id=0, has_side_effects=True, vmem_limit_bytes=58 << 20
        ),
        name="mix",
    )(state, slab)
    moment = jnp.sum(moments) / float(levels * levels * columns * groups * levels * THIRD)

    loads = column_load.astype(f32)
    offset = me * local_one
    levels_one = (offset + jnp.arange(local_one)).astype(f32)
    levels_two = jnp.arange(levels).astype(f32)
    phase_one = (kerr_rates[0] * levels_one)[:, None] * loads[None, :]
    phase_two = (kerr_rates[1] * levels_two)[:, None] * loads[None, :]
    one = jnp.stack([jnp.cos(phase_one), jnp.sin(phase_one)])
    two = jnp.stack([jnp.cos(phase_two), jnp.sin(phase_two)])
    tile_columns = min(columns, 512)
    evolved = pl.pallas_call(
        functools.partial(evolve_kernel, levels, packed),
        grid=(columns // tile_columns,),
        out_shape=jax.ShapeDtypeStruct((2, local_one, levels, columns), f32),
        in_specs=[
            pl.BlockSpec(memory_space=pltpu.SMEM),
            pl.BlockSpec((2, local_one, tile_columns), lambda c: (0, 0, c)),
            pl.BlockSpec((2, levels, tile_columns), lambda c: (0, 0, c)),
            pl.BlockSpec((results, 2, local_one, levels, tile_columns), lambda c: (0, 0, 0, 0, c)),
            pl.BlockSpec((2, 2, 5, BAND, tile_columns), lambda c: (0, 0, 0, 0, c)),
        ],
        out_specs=pl.BlockSpec((2, local_one, levels, tile_columns), lambda c: (0, 0, 0, c)),
        compiler_params=pltpu.CompilerParams(vmem_limit_bytes=48 << 20),
        name="evolve",
    )(offset.reshape(1).astype(jnp.int32), one, two, home, diag)
    return (evolved, moment.reshape(1))


def solution(mesh):
    placed = (P(None, "pairs", None, "cols"), P(None, None, "cols"), P(), P("cols"))
    return jax.shard_map(
        local,
        mesh=mesh,
        in_specs=placed,
        out_specs=(P(None, "pairs", None, "cols"), P()),
        check_vma=False,
    )
```

```python
import functools

import jax
import jax.numpy as jnp
from jax import lax
from jax.experimental import pallas as pl
from jax.experimental.pallas import tpu as pltpu
from jax.sharding import PartitionSpec as P

THIRD = 64
MEMB = 128
WINDOW = 2
BAND = 8
LANES = 128
CHUNK = 256
MESH = pl.DeviceIdType.MESH


def band_count(group, p, local_one, levels):
    lower = lax.div(levels - 1 - p * local_one, BAND) + 1
    upper = levels // BAND - lax.div(levels + 1 - local_one - p * local_one, BAND)
    return jnp.where(group == 0, lower, upper)


def turned(tile, by):
    return jnp.concatenate([tile[BAND - by :], tile[: BAND - by]], axis=0)


def joined(take, k, group):
    ids = lax.broadcasted_iota(jnp.int32, take(0).shape, 0)
    kept, moved = take(k), turned(take(BAND - k), BAND - k)
    return jnp.where((ids < BAND - k) == (group == 0), kept, moved)


def mix_kernel(
    count, groups, levels,
    state_ref, slab_ref, home_ref, moment_ref, diag_ref,
    rows, slabs, planes, factors, own_moment, pair_moments, col_moments,
    go_sem, come_sem, back_sem, home_sem, own_sem, own_home_sem,
    slab_send, slab_recv, slab_own, mp_send, mp_recv, mc_send, mc_recv,
    stage=None, tiles=None, packs=None, stage_sem=None, pack_go_sem=None, pack_come_sem=None,
    pack_back_sem=None, pack_home_sem=None, pack_own_sem=None, pack_own_home_sem=None,
):
    packed = stage is not None
    me = lax.axis_index("pairs")
    mine = lax.axis_index("cols")
    local_one, columns = state_ref.shape[1], state_ref.shape[3]
    half = count // 2
    width = columns // half
    chunk = min(CHUNK, width)
    chunks = width // chunk
    bands = levels // BAND
    depth = slab_ref.shape[1]
    group = lax.div(me, half)

    if packed:
        meet = pl.ds(pl.multiple_of(levels - BAND - me * BAND, BAND), BAND)
        staged = pltpu.make_async_copy(state_ref.at[:, :, meet, :], stage, stage_sem)
        staged.start()
    barrier = pltpu.get_barrier_semaphore()

    def greet_pair(k, carry):
        pl.semaphore_signal(
            barrier, inc=1, device_id=(lax.rem(me + k, count), mine), device_id_type=MESH
        )
        return carry

    def greet_col(k, carry):
        pl.semaphore_signal(
            barrier, inc=1, device_id=(me, lax.rem(mine + k, groups)), device_id_type=MESH
        )
        return carry

    lax.fori_loop(1, count, greet_pair, 0)
    lax.fori_loop(1, groups, greet_col, 0)
    pl.semaphore_wait(barrier, count + groups - 2)

    def at_home(ref, owner, c, n):
        first = lax.div(owner, half) * (levels - n * BAND)
        start = lax.rem(owner, half) * width + c * chunk
        return ref.at[
            :, :, pl.ds(pl.multiple_of(first, BAND), n * BAND),
            pl.ds(pl.multiple_of(start, LANES), chunk),
        ]

    def at_owner(owner, p, c, n):
        first = lax.div(owner, half) * (levels - n * BAND)
        return rows.at[
            :, pl.ds(p * local_one, local_one), pl.ds(pl.multiple_of(first, BAND), n * BAND),
            pl.ds(pl.multiple_of(c * chunk, LANES), chunk),
        ]

    def sized(owner, p, act):
        found = band_count(lax.div(owner, half), p, local_one, levels) - int(packed)
        for n in range(1, bands + 1):
            @pl.when(found == n)
            def _():
                act(n)

    def result_of(owner):
        return home_ref.at[0 if packed else lax.div(owner, half)]

    def go(p, owner, c, n):
        return pltpu.make_async_remote_copy(
            src_ref=at_home(state_ref, owner, c, n),
            dst_ref=at_owner(owner, p, c, n),
            send_sem=go_sem.at[owner, c],
            recv_sem=come_sem.at[p, c],
            device_id=(owner, mine),
            device_id_type=MESH,
        )

    def back(owner, p, c, n):
        return pltpu.make_async_remote_copy(
            src_ref=at_owner(owner, p, c, n),
            dst_ref=at_home(result_of(owner), owner, c, n),
            send_sem=back_sem.at[p, c],
            recv_sem=home_sem.at[owner, c],
            device_id=(p, mine),
            device_id_type=MESH,
        )

    def own_go(c, n):
        return pltpu.make_async_copy(
            at_home(state_ref, me, c, n), at_owner(me, me, c, n), own_sem.at[c]
        )

    def own_back(c, n):
        return pltpu.make_async_copy(
            at_owner(me, me, c, n), at_home(result_of(me), me, c, n), own_home_sem.at[c]
        )

    def columns_of(owner, c):
        start = lax.rem(owner, half) * width + c * chunk
        return pl.ds(pl.multiple_of(start, LANES), chunk)

    def pack_tiles(owner, act):
        if not packed:
            return
        for which in range(2):
            @pl.when(lax.div(owner, half) == which)
            def _():
                act(which)

    def pack_at_owner(p, c, which):
        return packs.at[
            :, p, pl.ds(0, 5 - which), :, pl.ds(pl.multiple_of(c * chunk, LANES), chunk)
        ]

    def pack_at_home(owner, c, which):
        return tiles.at[:, pl.ds(5 * which, 5 - which), :, columns_of(owner, c)]

    def pack_result(owner, c, which):
        return diag_ref.at[which, :, pl.ds(0, 5 - which), :, columns_of(owner, c)]

    def pack_go(p, owner, c, which):
        return pltpu.make_async_remote_copy(
            src_ref=pack_at_home(owner, c, which),
            dst_ref=pack_at_owner(p, c, which),
            send_sem=pack_go_sem.at[owner, c],
            recv_sem=pack_come_sem.at[p, c],
            device_id=(owner, mine),
            device_id_type=MESH,
        )

    def pack_back(owner, p, c, which):
        return pltpu.make_async_remote_copy(
            src_ref=pack_at_owner(p, c, which),
            dst_ref=pack_result(owner, c, which),
            send_sem=pack_back_sem.at[p, c],
            recv_sem=pack_home_sem.at[owner, c],
            device_id=(p, mine),
            device_id_type=MESH,
        )

    def pack_own_go(c, which):
        return pltpu.make_async_copy(
            pack_at_home(me, c, which), pack_at_owner(me, c, which), pack_own_sem.at[c]
        )

    def pack_own_back(c, which):
        return pltpu.make_async_copy(
            pack_at_owner(me, c, which), pack_result(me, c, which), pack_own_home_sem.at[c]
        )

    def peers(act):
        def body(k, carry):
            act(lax.rem(me + k, count))
            return carry

        lax.fori_loop(1, count, body, 0)

    def col_peers(act):
        def body(k, carry):
            act(lax.rem(mine + k, groups))
            return carry

        lax.fori_loop(1, groups, body, 0)

    def slab_place(col):
        return slabs.at[:, pl.ds(pl.multiple_of(col * depth, BAND), depth), :]

    def slab(source, dest):
        return pltpu.make_async_remote_copy(
            src_ref=slab_ref,
            dst_ref=slab_place(source),
            send_sem=slab_send.at[dest],
            recv_sem=slab_recv.at[source],
            device_id=(me, dest),
            device_id_type=MESH,
        )

    slab_here = pltpu.make_async_copy(slab_ref, slab_place(mine), slab_own)
    col_peers(lambda dest: slab(mine, dest).start())
    slab_here.start()

    if packed:
        staged.wait()

        def pack(c, carry):
            lanes = pl.ds(pl.multiple_of(c * chunk, LANES), chunk)
            for part in range(2):
                def take(i):
                    return stage[part, i, :, lanes]

                tiles[part, 0, :, lanes] = take(0)
                for k in range(1, 4):
                    for which in range(2):
                        tiles[part, 4 * which + k, :, lanes] = joined(take, k, which)
                for which in range(2):
                    tiles[part, 4 + 4 * which, :, lanes] = take(4)
            return carry

        lax.fori_loop(0, columns // chunk, pack, 0)

    def send_chunk(c, carry):
        def send(dest):
            sized(dest, me, lambda n: go(me, dest, c, n).start())
            pack_tiles(dest, lambda which: pack_go(me, dest, c, which).start())

        peers(send)
        sized(me, me, lambda n: own_go(c, n).start())
        pack_tiles(me, lambda which: pack_own_go(c, which).start())
        return carry

    lax.fori_loop(0, chunks, send_chunk, 0)

    col_peers(lambda source: slab(source, mine).wait_recv())
    slab_here.wait()

    def turn(i, carry):
        wide = jnp.concatenate(
            [slabs[i], jnp.zeros((LANES - levels, LANES), jnp.float32)], axis=0
        )
        planes[0, pl.ds(i, 2 * levels, stride=levels), :] = wide.T
        return carry

    lax.fori_loop(0, levels, turn, 0)

    def split(t, carry):
        start = pl.multiple_of((group * levels + t) * levels, BAND)
        whole = planes[0, pl.ds(start, levels), :][:, :levels]
        high = whole.astype(jnp.bfloat16)
        low = (whole - high.astype(jnp.float32)).astype(jnp.bfloat16)
        factors[t] = jnp.concatenate([high, high, low], axis=1)
        return carry

    lax.fori_loop(0, levels, split, 0)

    def clear(i, carry):
        start = pl.multiple_of(i * levels, BAND)
        for part in range(2):
            planes[part, pl.ds(start, levels), :] = jnp.zeros((levels, LANES), jnp.float32)
        return carry

    lax.fori_loop(0, 2 * levels, clear, 0)
    own_moment[...] = jnp.zeros_like(own_moment)
    row_ids = lax.broadcasted_iota(jnp.int32, (levels, 2 * LANES), 0)

    def both(act):
        @pl.when(group == 0)
        def _():
            def level(n1, carry):
                act(n1, pl.ds(n1 * (levels + 1), levels, stride=levels))
                return carry

            lax.fori_loop(0, levels, level, 0, unroll=2)

        @pl.when(group == 1)
        def _():
            def level(n1, carry):
                act(n1, pl.ds(n1 * levels + levels - 1, levels, stride=levels - 1))
                return carry

            lax.fori_loop(0, levels, level, 0, unroll=2)

    def mix_tile(start_column):
        lanes = pl.ds(pl.multiple_of(start_column, LANES), LANES)

        def put(n1, where):
            for part in range(2):
                planes[part, where, :] = rows[part, n1, :, lanes]

        def get(n1, where):
            for part in range(2):
                rows[part, n1, :, lanes] = planes[part, where, :]

        both(put)

        def sector(t, total):
            start = pl.multiple_of((group * levels + t) * levels, BAND)
            block = jnp.concatenate(
                [planes[0, pl.ds(start, levels), :], planes[1, pl.ds(start, levels), :]], axis=1
            )
            high = block.astype(jnp.bfloat16)
            low = (block - high.astype(jnp.float32)).astype(jnp.bfloat16)
            found = jnp.dot(
                factors[t],
                jnp.concatenate([high, low, high], axis=0),
                preferred_element_type=jnp.float32,
            )
            size = jnp.where(group == 0, t + 1, levels - 1 - t)
            first = jnp.where(group == 0, 0, t + 1)
            found = jnp.where(row_ids < size, found, 0.0)
            planes[0, pl.ds(start, levels), :] = found[:, :LANES]
            planes[1, pl.ds(start, levels), :] = found[:, LANES:]
            term = (row_ids + (first + 1)).astype(jnp.float32) * found * found
            for band in range(bands):
                total = total + term[band * BAND : (band + 1) * BAND]
            return total

        total = lax.fori_loop(
            0, levels, sector, jnp.zeros((BAND, 2 * LANES), jnp.float32), unroll=4
        )
        column = mine * columns + lax.rem(me, half) * width + start_column
        third = lax.div(column, MEMB * WINDOW).astype(jnp.float32)
        own_moment[...] += (third + 1.0) * (total[:, :LANES] + total[:, LANES:])
        both(get)

    def mix_chunk(c, carry):
        def arrive(source):
            sized(me, source, lambda n: go(source, me, c, n).wait_recv())
            pack_tiles(me, lambda which: pack_go(source, me, c, which).wait_recv())

        peers(arrive)
        sized(me, me, lambda n: own_go(c, n).wait())
        pack_tiles(me, lambda which: pack_own_go(c, which).wait())
        lanes = pl.ds(pl.multiple_of(c * chunk, LANES), chunk)

        def place(p, i, part):
            band = pl.ds(pl.multiple_of(levels - BAND - p * BAND, BAND), BAND)
            return (part, p * BAND + i, band, lanes)

        def unpack(p, carry):
            for part in range(2):
                rows[place(p, 0, part)] = packs[part, p, 0, :, lanes]
                for k in range(1, 4):
                    found = packs[part, p, k - group, :, lanes]
                    rows[place(p, k, part)] = found
                    rows[place(p, BAND - k, part)] = turned(found, k)
                rows[place(p, 4, part)] = packs[part, p, 4 - group, :, lanes]
            return carry

        def repack(p, carry):
            for part in range(2):
                def take(i):
                    return rows[place(p, i, part)]

                packs[part, p, 0, :, lanes] = take(0)
                for k in range(1, 4):
                    packs[part, p, k - group, :, lanes] = joined(take, k, group)
                packs[part, p, 4 - group, :, lanes] = take(4)
            return carry

        if packed:
            lax.fori_loop(0, count, unpack, 0)

        def tile(i, carry):
            mix_tile(c * chunk + i * LANES)
            return carry

        lax.fori_loop(0, chunk // LANES, tile, 0)
        if packed:
            lax.fori_loop(0, count, repack, 0)

        def leave(p):
            sized(me, p, lambda n: back(me, p, c, n).start())
            pack_tiles(me, lambda which: pack_back(me, p, c, which).start())

        peers(leave)
        sized(me, me, lambda n: own_back(c, n).start())
        pack_tiles(me, lambda which: pack_own_back(c, which).start())
        return carry

    lax.fori_loop(0, chunks, mix_chunk, 0)

    def moment_pair(source, dest):
        return pltpu.make_async_remote_copy(
            src_ref=own_moment, dst_ref=pair_moments.at[source],
            send_sem=mp_send.at[dest], recv_sem=mp_recv.at[source],
            device_id=(dest, mine), device_id_type=MESH,
        )

    def moment_col(source, dest):
        return pltpu.make_async_remote_copy(
            src_ref=moment_ref, dst_ref=col_moments.at[source],
            send_sem=mc_send.at[dest], recv_sem=mc_recv.at[source],
            device_id=(me, dest), device_id_type=MESH,
        )

    peers(lambda dest: moment_pair(me, dest).start())
    pair_moments[me] = own_moment[...]
    peers(lambda source: moment_pair(source, me).wait_recv())
    moment_ref[...] = jnp.sum(pair_moments[...], axis=0)
    col_peers(lambda dest: moment_col(mine, dest).start())
    col_moments[mine] = moment_ref[...]
    col_peers(lambda source: moment_col(source, mine).wait_recv())
    col_peers(lambda dest: moment_col(mine, dest).wait_send())
    moment_ref[...] = jnp.sum(col_moments[...], axis=0)

    peers(lambda dest: moment_pair(me, dest).wait_send())
    col_peers(lambda dest: slab(mine, dest).wait_send())

    def finish(c, carry):
        peers(lambda dest: sized(dest, me, lambda n: go(me, dest, c, n).wait_send()))
        peers(lambda p: sized(me, p, lambda n: back(me, p, c, n).wait_send()))
        peers(lambda owner: sized(owner, me, lambda n: back(owner, me, c, n).wait_recv()))
        sized(me, me, lambda n: own_back(c, n).wait())

        def finish_pack(peer):
            pack_tiles(peer, lambda which: pack_go(me, peer, c, which).wait_send())
            pack_tiles(me, lambda which: pack_back(me, peer, c, which).wait_send())
            pack_tiles(peer, lambda which: pack_back(peer, me, c, which).wait_recv())

        if packed:
            peers(finish_pack)
            pack_tiles(me, lambda which: pack_own_back(c, which).wait())
        return carry

    lax.fori_loop(0, chunks, finish, 0)


def evolve_kernel(levels, packed, offset_ref, one_ref, two_ref, home_ref, diag_ref, evolved_ref):
    offset = offset_ref[0]
    local_one = home_ref.shape[2]
    shape = home_ref.shape[3:]
    n2 = lax.broadcasted_iota(jnp.int32, shape, 0)
    cos_two, sin_two = two_ref[0], two_ref[1]
    for i in range(local_one):
        real, imag = home_ref[0, 0, i], home_ref[0, 1, i]
        if not packed:
            lower = n2 + (offset + i) < levels
            real = jnp.where(lower, real, home_ref[1, 0, i])
            imag = jnp.where(lower, imag, home_ref[1, 1, i])
        cos_one, sin_one = one_ref[0, i : i + 1, :], one_ref[1, i : i + 1, :]
        cosine = cos_one * cos_two - sin_one * sin_two
        sine = sin_one * cos_two + cos_one * sin_two
        evolved_ref[0, i] = cosine * real - sine * imag
        evolved_ref[1, i] = sine * real + cosine * imag
    if not packed:
        return
    band = pl.ds(pl.multiple_of(levels - BAND - offset, BAND), BAND)
    cos_two, sin_two = two_ref[0, band, :], two_ref[1, band, :]
    ids = lax.broadcasted_iota(jnp.int32, cos_two.shape, 0)
    for i in range(local_one):
        k = min(i, BAND - i)
        found = []
        for part in range(2):
            lower = diag_ref[0, part, k]
            if i == 0:
                found.append(lower)
                continue
            upper = diag_ref[1, part, k - 1]
            if i <= 4:
                found.append(jnp.where(ids < BAND - k, lower, upper))
            else:
                found.append(turned(jnp.where(ids < BAND - k, upper, lower), k))
        real, imag = found
        cos_one, sin_one = one_ref[0, i : i + 1, :], one_ref[1, i : i + 1, :]
        cosine = cos_one * cos_two - sin_one * sin_two
        sine = sin_one * cos_two + cos_one * sin_two
        evolved_ref[0, i, band, :] = cosine * real - sine * imag
        evolved_ref[1, i, band, :] = sine * real + cosine * imag


def local(state, sector_mix, kerr_rates, column_load):
    count = lax.axis_size("pairs")
    groups = lax.axis_size("cols")
    me = lax.axis_index("pairs")
    _, local_one, levels, columns = state.shape
    half = count // 2
    width = columns // half
    chunks = width // min(CHUNK, width)
    f32 = jnp.float32
    anywhere = pl.BlockSpec(memory_space=pl.ANY)
    tile = (BAND, LANES)
    dma = pltpu.SemaphoreType.DMA

    slab = jnp.pad(
        jnp.transpose(sector_mix, (1, 2, 0)),
        ((0, 0), (0, 0), (0, 2 * levels - sector_mix.shape[0])),
    )
    packed = local_one == BAND
    results = 1 if packed else 2
    extra = [
        pltpu.VMEM((2, local_one, BAND, columns), f32),
        pltpu.VMEM((2, 9, BAND, columns), f32),
        pltpu.VMEM((2, count, 5, BAND, width), f32),
        dma,
        dma((count, chunks)), dma((count, chunks)),
        dma((count, chunks)), dma((count, chunks)),
        dma((chunks,)), dma((chunks,)),
    ]
    home, moments, diag = pl.pallas_call(
        functools.partial(mix_kernel, count, groups, levels),
        out_shape=(
            jax.ShapeDtypeStruct((results, 2, local_one, levels, columns), f32),
            jax.ShapeDtypeStruct(tile, f32),
            jax.ShapeDtypeStruct((2, 2, 5, BAND, columns), f32),
        ),
        in_specs=[anywhere, anywhere],
        out_specs=(anywhere, pl.BlockSpec(memory_space=pltpu.VMEM), anywhere),
        scratch_shapes=[
            pltpu.VMEM((2, levels, levels, width), f32),
            pltpu.VMEM((levels, levels, 2 * levels), f32),
            pltpu.VMEM((2, 2 * levels * levels, LANES), f32),
            pltpu.VMEM((levels, levels, 3 * levels), jnp.bfloat16),
            pltpu.VMEM(tile, f32),
            pltpu.VMEM((count,) + tile, f32),
            pltpu.VMEM((groups,) + tile, f32),
            dma((count, chunks)), dma((count, chunks)),
            dma((count, chunks)), dma((count, chunks)),
            dma((chunks,)), dma((chunks,)),
            dma((groups,)), dma((groups,)), dma,
            dma((count,)), dma((count,)), dma((groups,)), dma((groups,)),
        ] + (extra if packed else []),
        compiler_params=pltpu.CompilerParams(
            collective_id=0, has_side_effects=True, vmem_limit_bytes=58 << 20
        ),
        name="mix",
    )(state, slab)
    moment = jnp.sum(moments) / float(levels * levels * columns * groups * levels * THIRD)

    loads = column_load.astype(f32)
    offset = me * local_one
    levels_one = (offset + jnp.arange(local_one)).astype(f32)
    levels_two = jnp.arange(levels).astype(f32)
    phase_one = (kerr_rates[0] * levels_one)[:, None] * loads[None, :]
    phase_two = (kerr_rates[1] * levels_two)[:, None] * loads[None, :]
    one = jnp.stack([jnp.cos(phase_one), jnp.sin(phase_one)])
    two = jnp.stack([jnp.cos(phase_two), jnp.sin(phase_two)])
    tile_columns = min(columns, 512)
    evolved = pl.pallas_call(
        functools.partial(evolve_kernel, levels, packed),
        grid=(columns // tile_columns,),
        out_shape=jax.ShapeDtypeStruct((2, local_one, levels, columns), f32),
        in_specs=[
            pl.BlockSpec(memory_space=pltpu.SMEM),
            pl.BlockSpec((2, local_one, tile_columns), lambda c: (0, 0, c)),
            pl.BlockSpec((2, levels, tile_columns), lambda c: (0, 0, c)),
            pl.BlockSpec((results, 2, local_one, levels, tile_columns), lambda c: (0, 0, 0, 0, c)),
            pl.BlockSpec((2, 2, 5, BAND, tile_columns), lambda c: (0, 0, 0, 0, c)),
        ],
        out_specs=pl.BlockSpec((2, local_one, levels, tile_columns), lambda c: (0, 0, 0, c)),
        compiler_params=pltpu.CompilerParams(vmem_limit_bytes=48 << 20),
        name="evolve",
    )(offset.reshape(1).astype(jnp.int32), one, two, home, diag)
    return (evolved, moment.reshape(1))


def solution(mesh):
    placed = (P(None, "pairs", None, "cols"), P(None, None, "cols"), P(), P("cols"))
    return jax.shard_map(
        local,
        mesh=mesh,
        in_specs=placed,
        out_specs=(P(None, "pairs", None, "cols"), P()),
        check_vma=False,
    )
```
